512 devices in a mesh: band: 64 (over x, y, z_lo), dom: 8 (over z_hi, core).
Axes of the slice: x: 4, y: 8, z: 8 (z_hi: 4, z_lo: 2; z = z_hi * 2 + z_lo), core: 2. Of those that a mesh axis runs over, the one named last changes fastest.
Arguments:
- orbitals: bfloat16 [128, 48, 32, 128], P('band', 'dom'), may hold values from -6.5 to 6.5
- potential: float32 [48, 32, 128], P('dom'), may hold values from -0.3 to 3.3
Outputs:
- correlation: float32 [128, 128], P('band')
- projected: float32 [128, 128], P('band')
The draws below stay inside these ranges and needn't reach their ends.
All inputs are finite; a program needn't handle non-finite values.
Results may differ from the reference program's by a relative error of at most 0.00045.
Values may be sent and summed in bfloat16 or wider, within the bound.
A program may use at most 64 MiB of HBM per device.

```python
import math
import jax
import jax.numpy as jnp
from jax import lax

NORB = 128
NX = 128
NY = 32
CZ = 6
NZ = 48


def draw_orbitals(key, part):
    key = jax.random.fold_in(key, 11)
    key_noise, key_weight, key_phase = jax.random.split(key, 3)
    random_part = jnp.clip(jax.random.normal(key_noise, (NORB, NZ, NY, NX), jnp.float32), -4.0, 4.0)
    weights = jnp.clip(jax.random.normal(key_weight, (NORB,), jnp.float32), -3.0, 3.0)
    phases = jax.random.uniform(key_phase, (3,), jnp.float32, 0.0, 2.0 * math.pi)
    zpos = jnp.arange(NZ).astype(jnp.float32)
    ypos = jnp.arange(NY).astype(jnp.float32)
    xpos = jnp.arange(NX).astype(jnp.float32)
    along_z = (0.4 + 1.2 * zpos / NZ) * (1.0 + 0.5 * jnp.cos(math.pi * zpos / CZ + phases[0]))
    along_y = jnp.cos(2.0 * math.pi * ypos / NY + phases[1])
    along_x = jnp.cos(2.0 * math.pi * xpos / NX + phases[2])
    shared = along_z[:, None, None] * along_y[None, :, None] * along_x[None, None, :]
    return (random_part + 0.3 * weights[:, None, None, None] * shared[None]).astype(jnp.bfloat16)


def draw_potential(key, part):
    key = jax.random.fold_in(key, 23)
    key_rough, key_phase = jax.random.split(key, 2)
    rough = jax.random.uniform(key_rough, (NZ, NY, NX), jnp.float32, -1.0, 1.0)
    phases = jax.random.uniform(key_phase, (2,), jnp.float32, 0.0, 2.0 * math.pi)
    zpos = jnp.arange(NZ).astype(jnp.float32)
    ypos = jnp.arange(NY).astype(jnp.float32)
    smooth = jnp.cos(2.0 * math.pi * zpos / NZ + phases[0])[:, None, None] * jnp.cos(2.0 * math.pi * ypos / NY + phases[1])[None, :, None]
    return 1.5 + 0.6 * rough + 1.2 * smooth


def setup_inputs(seed: int = 0) -> dict:
    splits = jax.random.split(jax.random.key(seed), 3)
    orbitals = draw_orbitals(jax.random.fold_in(splits[2], 71), 0)
    potential = draw_potential(jax.random.fold_in(splits[2], 71), 0)
    return {"orbitals": orbitals, "potential": potential}


STENCIL = (-5369.0 / 1800.0, 12.0 / 7.0, -15.0 / 56.0, 10.0 / 189.0, -1.0 / 112.0, 2.0 / 1925.0, -1.0 / 16632.0)
CENTER = 8.5
SCALE = 1.0 / 5.5


def hamilton(field, padded, potential):
    planes = field.shape[-3]
    summed = (3.0 * STENCIL[0]) * field
    for offset in range(1, 7):
        along_y = jnp.roll(field, offset, -2) + jnp.roll(field, -offset, -2)
        along_x = jnp.roll(field, offset, -1) + jnp.roll(field, -offset, -1)
        upper = lax.slice_in_dim(padded, 6 + offset, 6 + offset + planes, axis=padded.ndim - 3)
        lower = lax.slice_in_dim(padded, 6 - offset, 6 - offset + planes, axis=padded.ndim - 3)
        summed = summed + STENCIL[offset] * (along_y + along_x + (upper + lower))
    return -0.5 * summed + potential * field


def apply_full(field, potential):
    padded = jnp.pad(field, ((6, 6), (0, 0), (0, 0)))
    return hamilton(field, padded, potential)


def reference(orbitals, potential):
    def filter_one(orbital):
        first = orbital.astype(jnp.float32)
        second = (apply_full(first, potential) - CENTER * first) * SCALE
        third = 2.0 * (apply_full(second, potential) - CENTER * second) * SCALE - first
        fourth = 2.0 * (apply_full(third, potential) - CENTER * third) * SCALE - second
        image = apply_full(fourth, potential)
        return fourth.astype(jnp.bfloat16), image.astype(jnp.bfloat16)

    filtered, image = lax.map(filter_one, orbitals)
    count = orbitals.shape[0]
    flat_panel = filtered.reshape(count, -1)
    flat_image = image.reshape(count, -1)
    cell_scale = 1.0 / (NX * NY * NZ)
    correlation = jnp.dot(flat_panel, flat_panel.T, preferred_element_type=jnp.float32) * cell_scale
    projected = jnp.dot(flat_image, flat_panel.T, preferred_element_type=jnp.float32) * cell_scale
    return correlation, projected
```

```python
import functools

import jax
import jax.numpy as jnp
from jax import lax
from jax.experimental import pallas as pl
from jax.experimental.pallas import tpu as pltpu
from jax.sharding import PartitionSpec as P

STENCIL = (
    -5369.0 / 1800.0,
    12.0 / 7.0,
    -15.0 / 56.0,
    10.0 / 189.0,
    -1.0 / 112.0,
    2.0 / 1925.0,
    -1.0 / 16632.0,
)
HALF = tuple(-0.5 * w for w in STENCIL)
CENTER = 8.5
SCALE = 1.0 / 5.5
MESH = pl.DeviceIdType.MESH
NBAND, NDOM = 64, 8
PLANES, ROWS, LANES = 6, 32, 128
CHUNKS = 24
NORB = 128


def owner_band(k, core):
    third, y = k // 8, k % 8
    x = third + core * (3 - 2 * third)
    return x * 16 + y * 2 + third % 2


def kernel(
    orb_hbm, pot_hbm, out_ref,
    slab, pot, halo, fields, acc, filt_out, img_out, filt_in, img_in, wide, filt_mat,
    corr_out, proj_out, corr_in, proj_in, corr_dom, proj_dom,
    load_sem, hsend, hrecv, fsend, frecv, isend, irecv, csend, crecv, psend, precv, dsend, drecv, esend, erecv,
):
    band = lax.axis_index("band")
    dom = lax.axis_index("dom")
    core = dom % 2
    x, zl = band // 16, band % 2
    third = x + core * (3 - 2 * x)
    my_chunk = third * 8 + (band // 2) % 8
    owner = jnp.logical_and(third < 3, zl == third % 2)

    def band_peer(k):
        return (lax.rem(band + k, NBAND), dom)

    def dom_peer(k):
        return (band, lax.rem(dom + k, NDOM))

    barrier = pltpu.get_barrier_semaphore()

    def greet_dom(k, _):
        pl.semaphore_signal(barrier, inc=1, device_id=dom_peer(k), device_id_type=MESH)
        return 0

    def greet_band(k, _):
        pl.semaphore_signal(barrier, inc=1, device_id=band_peer(k), device_id_type=MESH)
        return 0

    lax.fori_loop(1, NBAND, greet_band, 0)
    lax.fori_loop(1, NDOM, greet_dom, 0)

    load_orb = pltpu.make_async_copy(orb_hbm, slab.at[0], load_sem.at[0])
    load_pot = pltpu.make_async_copy(pot_hbm, pot, load_sem.at[1])
    load_orb.start()
    load_pot.start()

    @pl.when(dom == 0)
    def _():
        for s in range(4):
            halo[s, 0] = jnp.zeros((2, PLANES, ROWS, LANES), jnp.bfloat16)

    @pl.when(dom == NDOM - 1)
    def _():
        for s in range(4):
            halo[s, 1] = jnp.zeros((2, PLANES, ROWS, LANES), jnp.bfloat16)

    load_orb.wait()
    load_pot.wait()

    def widen(o, _):
        fields[0, o] = slab[0, o].astype(jnp.float32)
        return 0

    lax.fori_loop(0, 2, widen, 0)

    def local_part(s, shift):
        def body(o, _):
            for p in range(PLANES):
                v = fields[s, o, p]
                total = (pot[p] + (3.0 * HALF[0] + shift)) * v
                for k in range(1, 7):
                    along_y = pltpu.roll(v, k, 0) + pltpu.roll(v, ROWS - k, 0)
                    along_x = pltpu.roll(v, k, 1) + pltpu.roll(v, LANES - k, 1)
                    total = total + HALF[k] * (along_y + along_x)
                for q in range(PLANES):
                    if q != p:
                        total = total + HALF[abs(p - q)] * fields[s, o, q]
                acc[o, p] = total
            return 0

        lax.fori_loop(0, 2, body, 0)

    def halo_copies(s):
        up = pltpu.make_async_remote_copy(
            src_ref=slab.at[s], dst_ref=halo.at[s, 0], send_sem=hsend.at[s, 0], recv_sem=hrecv.at[s, 0],
            device_id=dom_peer(1), device_id_type=MESH)
        down = pltpu.make_async_remote_copy(
            src_ref=slab.at[s], dst_ref=halo.at[s, 1], send_sem=hsend.at[s, 1], recv_sem=hrecv.at[s, 1],
            device_id=dom_peer(NDOM - 1), device_id_type=MESH)
        return up, down

    def halo_start(s):
        up, down = halo_copies(s)

        @pl.when(dom < NDOM - 1)
        def _():
            up.start()

        @pl.when(dom > 0)
        def _():
            down.start()

    def halo_wait(s):
        up, down = halo_copies(s)

        @pl.when(dom > 0)
        def _():
            up.wait_recv()

        @pl.when(dom < NDOM - 1)
        def _():
            down.wait_recv()

    def halo_sent(s):
        up, down = halo_copies(s)

        @pl.when(dom < NDOM - 1)
        def _():
            up.wait_send()

        @pl.when(dom > 0)
        def _():
            down.wait_send()

    def halo_part(s, store):
        def body(o, _):
            for h in range(2):
                rows = pl.ds(16 * h, 16)
                low = [halo[s, 0, o, j, rows, :].astype(jnp.float32) for j in range(PLANES)]
                high = [halo[s, 1, o, j, rows, :].astype(jnp.float32) for j in range(PLANES)]
                for p in range(PLANES):
                    total = acc[o, p, rows, :]
                    for j in range(p, PLANES):
                        total = total + HALF[p + 6 - j] * low[j]
                    for j in range(p + 1):
                        total = total + HALF[6 + j - p] * high[j]
                    store(o, p, h, rows, total)
            return 0

        lax.fori_loop(0, 2, body, 0)

    def store_field(s):
        def store(o, p, h, rows, total):
            if s == 1:
                value = SCALE * total
            else:
                value = (2.0 * SCALE) * total - fields[s - 2, o, p, rows, :]
            fields[s, o, p, rows, :] = value
            narrow = value.astype(jnp.bfloat16)
            slab[s, o, p, rows, :] = narrow
            if s == 3:
                for t in range(2):
                    filt_out[p * 4 + h * 2 + t, o] = value[8 * t:8 * t + 8].astype(jnp.bfloat16)

        return store

    def store_image(o, p, h, rows, total):
        for t in range(2):
            img_out[p * 4 + h * 2 + t, o] = total[8 * t:8 * t + 8].astype(jnp.bfloat16)

    def scatter(src, dst, send_sem, recv_sem):
        def body(i, _):
            k = lax.rem(i + band, CHUNKS)
            target = owner_band(k, core)

            @pl.when(target == band)
            def _():
                pltpu.make_async_copy(src.at[k], dst.at[band], recv_sem).start()

            @pl.when(target != band)
            def _():
                pltpu.make_async_remote_copy(
                    src_ref=src.at[k], dst_ref=dst.at[band], send_sem=send_sem, recv_sem=recv_sem,
                    device_id=(target, dom), device_id_type=MESH).start()

            return 0

        lax.fori_loop(0, CHUNKS, body, 0)

    def all_bytes(ref, sem):
        pltpu.make_async_copy(ref, ref, sem).wait()

    def scattered(src, send_sem):
        @pl.when(owner)
        def _():
            all_bytes(src.at[pl.ds(0, CHUNKS - 1)], send_sem)

        @pl.when(jnp.logical_not(owner))
        def _():
            all_bytes(src, send_sem)

    local_part(0, -CENTER)
    pl.semaphore_wait(barrier, NBAND + NDOM - 2)

    halo_start(0)
    halo_wait(0)
    halo_part(0, store_field(1))
    halo_start(1)
    local_part(1, -CENTER)
    halo_wait(1)
    halo_part(1, store_field(2))
    halo_start(2)
    local_part(2, -CENTER)
    halo_wait(2)
    halo_part(2, store_field(3))
    halo_start(3)
    scatter(filt_out, filt_in, fsend, frecv)
    local_part(3, 0.0)
    halo_wait(3)
    halo_part(3, store_image)
    scatter(img_out, img_in, isend, irecv)

    def by_row(src):
        wide[...] = src[...].astype(jnp.float32).reshape(NORB * 8, LANES)
        return [wide[pl.ds(r, NORB, stride=8), :].astype(jnp.bfloat16) for r in range(8)]

    def rows_back(total, out, dst, send_sem, recv_sem):
        for b in range(NBAND):
            out[b] = total[2 * b:2 * b + 2]

        def body(k, _):
            pltpu.make_async_remote_copy(
                src_ref=out.at[lax.rem(band + k, NBAND)], dst_ref=dst.at[my_chunk], send_sem=send_sem, recv_sem=recv_sem,
                device_id=band_peer(k), device_id_type=MESH).start()
            return 0

        lax.fori_loop(1, NBAND, body, 0)
        pltpu.make_async_copy(out.at[band], dst.at[my_chunk], recv_sem).start()

    contract = (((1,), (1,)), ((), ()))

    @pl.when(owner)
    def _():
        all_bytes(filt_in, frecv)
        filt = by_row(filt_in)
        for r in range(8):
            filt_mat[:, r * LANES:(r + 1) * LANES] = filt[r]
        mat = filt_mat[...]
        rows_back(lax.dot_general(mat, mat, contract, preferred_element_type=jnp.float32),
                  corr_out, corr_in, csend, crecv)
        all_bytes(img_in, irecv)
        img = jnp.concatenate(by_row(img_in), axis=1)
        rows_back(lax.dot_general(img, filt_mat[...], contract, preferred_element_type=jnp.float32),
                  proj_out, proj_in, psend, precv)

    def over_dom(src, dst, send_sem, recv_sem):
        dst[dom] = jnp.sum(src[...], axis=0)

        def body(k, _):
            pltpu.make_async_remote_copy(
                src_ref=dst.at[dom], dst_ref=dst.at[dom], send_sem=send_sem, recv_sem=recv_sem,
                device_id=dom_peer(k), device_id_type=MESH).start()
            return 0

        lax.fori_loop(1, NDOM, body, 0)

    all_bytes(corr_in, crecv)
    over_dom(corr_in, corr_dom, dsend, drecv)
    all_bytes(proj_in, precv)
    over_dom(proj_in, proj_dom, esend, erecv)
    most = pl.ds(0, NDOM - 1)
    all_bytes(corr_dom.at[most], drecv)
    all_bytes(proj_dom.at[most], erecv)
    cell_scale = 1.0 / (PLANES * ROWS * LANES * NDOM)
    out_ref[0] = jnp.sum(corr_dom[...], axis=0) * cell_scale
    out_ref[1] = jnp.sum(proj_dom[...], axis=0) * cell_scale

    for s in range(4):
        halo_sent(s)
    scattered(filt_out, fsend)
    scattered(img_out, isend)
    all_bytes(corr_dom.at[most], dsend)
    all_bytes(proj_dom.at[most], esend)

    @pl.when(owner)
    def _():
        all_bytes(corr_out.at[pl.ds(0, NBAND - 1)], csend)
        all_bytes(proj_out.at[pl.ds(0, NBAND - 1)], psend)


def per_device(orbitals, potential):
    bf16, f32 = jnp.bfloat16, jnp.float32
    dma = pltpu.SemaphoreType.DMA
    out = pl.pallas_call(
        kernel,
        out_shape=jax.ShapeDtypeStruct((2, 2, LANES), f32),
        in_specs=[pl.BlockSpec(memory_space=pl.ANY)] * 2,
        out_specs=pl.BlockSpec(memory_space=pltpu.VMEM),
        scratch_shapes=[
            pltpu.VMEM((4, 2, PLANES, ROWS, LANES), bf16),
            pltpu.VMEM((PLANES, ROWS, LANES), f32),
            pltpu.VMEM((4, 2, 2, PLANES, ROWS, LANES), bf16),
            pltpu.VMEM((4, 2, PLANES, ROWS, LANES), f32),
            pltpu.VMEM((2, PLANES, ROWS, LANES), f32),
            pltpu.VMEM((CHUNKS, 2, 8, LANES), bf16),
            pltpu.VMEM((CHUNKS, 2, 8, LANES), bf16),
            pltpu.VMEM((NBAND, 2, 8, LANES), bf16),
            pltpu.VMEM((NBAND, 2, 8, LANES), bf16),
            pltpu.VMEM((NORB * 8, LANES), f32),
            pltpu.VMEM((NORB, 8 * LANES), bf16),
            pltpu.VMEM((NBAND, 2, LANES), f32),
            pltpu.VMEM((NBAND, 2, LANES), f32),
            pltpu.VMEM((CHUNKS, 2, LANES), f32),
            pltpu.VMEM((CHUNKS, 2, LANES), f32),
            pltpu.VMEM((NDOM, 2, LANES), f32),
            pltpu.VMEM((NDOM, 2, LANES), f32),
            dma((2,)), dma((4, 2)), dma((4, 2)),
            dma, dma, dma, dma, dma, dma, dma, dma, dma, dma, dma, dma,
        ],
        compiler_params=pltpu.CompilerParams(collective_id=0, has_side_effects=True, vmem_limit_bytes=40 << 20),
    )(orbitals, potential)
    return out[0], out[1]


def solution(mesh):
    placed = (P("band", "dom", None, None), P("dom", None, None))
    return jax.shard_map(
        per_device,
        mesh=mesh,
        in_specs=placed,
        out_specs=(P("band", None), P("band", None)),
        check_vma=False,
    )
```

```python
import jax
import jax.numpy as jnp
from jax import lax
from jax.experimental import pallas as pl
from jax.experimental.pallas import tpu as pltpu
from jax.sharding import PartitionSpec as P

STENCIL = (
    -5369.0 / 1800.0,
    12.0 / 7.0,
    -15.0 / 56.0,
    10.0 / 189.0,
    -1.0 / 112.0,
    2.0 / 1925.0,
    -1.0 / 16632.0,
)
HALF = tuple(-0.5 * w for w in STENCIL)
CENTER = 8.5
SCALE = 1.0 / 5.5
MESH = pl.DeviceIdType.MESH
NBAND, NDOM = 64, 8
PLANES, ROWS, LANES = 6, 32, 128
CHUNKS = 24
NORB = 128


def image_step(t):
    return lax.rem(10 - t, 8)


def kernel(
    orb_hbm, pot_hbm, out_ref,
    slab, pot, halo, fields, acc, filt_out, img_out, filt_in, img_in, wide, filt_mat, rows_out, rows_in, sums,
    load_sem, hsend, hrecv, fsend, frecv, isend, irecv, rsend, rrecv, dsend, drecv,
):
    band = lax.axis_index("band")
    dom = lax.axis_index("dom")
    x, y, zl = band // 16, (band // 2) % 8, band % 2
    place = lax.rem(x + 7 - dom, 4)
    owner = place < 3
    my_chunk = (place * 2 + zl) * 4 + y % 4

    def band_at(x_, y_, zl_):
        return x_ * 16 + y_ * 2 + zl_

    def dom_peer(k):
        return (band, lax.rem(dom + k, NDOM))

    barrier = pltpu.get_barrier_semaphore()

    def greet_dom(k, _):
        pl.semaphore_signal(barrier, inc=1, device_id=dom_peer(k), device_id_type=MESH)
        return 0

    def greet_band(k, _):
        pl.semaphore_signal(barrier, inc=1, device_id=(lax.rem(band + k, NBAND), dom), device_id_type=MESH)
        return 0

    lax.fori_loop(1, NDOM, greet_dom, 0)
    lax.fori_loop(1, NBAND, greet_band, 0)

    load_orb = pltpu.make_async_copy(orb_hbm, slab.at[0], load_sem.at[0])
    load_pot = pltpu.make_async_copy(pot_hbm, pot, load_sem.at[1])
    load_orb.start()
    load_pot.start()

    @pl.when(dom == 0)
    def _():
        for s in range(4):
            halo[s, 0] = jnp.zeros((2, PLANES, ROWS, LANES), jnp.bfloat16)

    @pl.when(dom == NDOM - 1)
    def _():
        for s in range(4):
            halo[s, 1] = jnp.zeros((2, PLANES, ROWS, LANES), jnp.bfloat16)

    def local_part(s, shift):
        def body(o, _):
            for p in range(PLANES):
                v = fields[s, o, p]
                total = (pot[p] + (3.0 * HALF[0] + shift)) * v
                for k in range(1, 7):
                    along_y = pltpu.roll(v, k, 0) + pltpu.roll(v, ROWS - k, 0)
                    along_x = pltpu.roll(v, k, 1) + pltpu.roll(v, LANES - k, 1)
                    total = total + HALF[k] * (along_y + along_x)
                for q in range(PLANES):
                    if q != p:
                        total = total + HALF[abs(p - q)] * fields[s, o, q]
                acc[o, p] = total
            return 0

        lax.fori_loop(0, 2, body, 0)

    def halo_copies(s, o):
        source = orb_hbm.at[o] if s == 0 else slab.at[s, o]
        return [
            pltpu.make_async_remote_copy(
                src_ref=source, dst_ref=halo.at[s, side, o], send_sem=hsend.at[s, side, o], recv_sem=hrecv.at[s, side, o],
                device_id=dom_peer(step), device_id_type=MESH)
            for side, step in ((0, 1), (1, NDOM - 1))
        ]

    def halo_start(s, o):
        up, down = halo_copies(s, o)

        @pl.when(dom < NDOM - 1)
        def _():
            up.start()

        @pl.when(dom > 0)
        def _():
            down.start()

    def halo_wait(s, o):
        up, down = halo_copies(s, o)

        @pl.when(dom > 0)
        def _():
            up.wait_recv()

        @pl.when(dom < NDOM - 1)
        def _():
            down.wait_recv()

    def halo_sent(s, o):
        up, down = halo_copies(s, o)

        @pl.when(dom < NDOM - 1)
        def _():
            up.wait_send()

        @pl.when(dom > 0)
        def _():
            down.wait_send()

    def halo_part(s, o, store):
        for h in range(2):
            rows = pl.ds(16 * h, 16)
            low = [halo[s, 0, o, j, rows, :].astype(jnp.float32) for j in range(PLANES)]
            high = [halo[s, 1, o, j, rows, :].astype(jnp.float32) for j in range(PLANES)]
            for p in range(PLANES):
                total = acc[o, p, rows, :]
                for j in range(p, PLANES):
                    total = total + HALF[p + 6 - j] * low[j]
                for j in range(p + 1):
                    total = total + HALF[6 + j - p] * high[j]
                store(o, p, h, rows, total)

    def store_field(s):
        def store(o, p, h, rows, total):
            if s == 1:
                value = SCALE * total
            else:
                value = (2.0 * SCALE) * total - fields[s - 2, o, p, rows, :]
            fields[s, o, p, rows, :] = value
            slab[s, o, p, rows, :] = value.astype(jnp.bfloat16)
            if s == 3:
                for t in range(2):
                    filt_out[p * 4 + h * 2 + t, o] = value[8 * t:8 * t + 8].astype(jnp.bfloat16)

        return store

    def store_image(o, p, h, rows, total):
        for t in range(2):
            img_out[p * 4 + h * 2 + t, o] = total[8 * t:8 * t + 8].astype(jnp.bfloat16)

    def send(src, dst, target, send_sem, recv_sem):
        pltpu.make_async_remote_copy(
            src_ref=src, dst_ref=dst, send_sem=send_sem, recv_sem=recv_sem,
            device_id=(target, dom), device_id_type=MESH).start()

    def send_or_keep(src, dst, target, send_sem, recv_sem):
        @pl.when(target == band)
        def _():
            pltpu.make_async_copy(src, dst, recv_sem).start()

        @pl.when(target != band)
        def _():
            send(src, dst, target, send_sem, recv_sem)

    def to_owners(src, dst, slot_of, step_of, steps, send_sem, recv_sem):
        def body(i, _):
            step = step_of(i // 6)
            r = i % 6
            place_, zl_ = r // 2, r % 2
            y_ = lax.rem(y + step, 8)
            k = r * 4 + y_ % 4
            target = band_at(lax.rem(dom + 1 + place_, 4), y_, zl_)
            send_or_keep(src.at[k], dst.at[slot_of(step)], target, send_sem, recv_sem)
            return 0

        lax.fori_loop(0, 6 * steps, body, 0)

    def all_bytes(ref, sem):
        pltpu.make_async_copy(ref, ref, sem).wait()

    pl.semaphore_wait(barrier, NBAND + NDOM - 2)
    for o in range(2):
        halo_start(0, o)
    load_orb.wait()
    load_pot.wait()

    def widen(o, _):
        fields[0, o] = slab[0, o].astype(jnp.float32)
        return 0

    lax.fori_loop(0, 2, widen, 0)
    local_part(0, -CENTER)
    for s in range(3):
        for o in range(2):
            halo_wait(s, o)
            halo_part(s, o, store_field(s + 1))
            halo_start(s + 1, o)
        if s == 2:
            to_owners(filt_out, filt_in, lambda step: band, lambda t: 4 + ((t + 1) // 2) * (1 - 2 * (t % 2)), 8, fsend, frecv)
        local_part(s + 1, -CENTER if s < 2 else 0.0)
    for o in range(2):
        halo_wait(3, o)
        halo_part(3, o, store_image)
    to_owners(img_out, img_in, lambda step: x * 8 + lax.rem(10 - step, 8) * 2 + zl, image_step, 4, isend, irecv)

    def by_row(src, count):
        rows = wide.at[pl.ds(0, count * 8)]
        rows[...] = src[...].astype(jnp.float32).reshape(count * 8, LANES)
        return [wide[pl.ds(r, count, stride=8), :].astype(jnp.bfloat16) for r in range(8)]

    contract = (((1,), (1,)), ((), ()))

    @pl.when(owner)
    def _():
        all_bytes(filt_in, frecv)
        filt = by_row(filt_in, NORB)
        for r in range(8):
            filt_mat[:, r * LANES:(r + 1) * LANES] = filt[r]
        mat = filt_mat[...]
        corr = lax.dot_general(mat, mat, contract, preferred_element_type=jnp.float32)
        for b in range(NBAND):
            rows_out[b, 0] = corr[2 * b:2 * b + 2]
        all_bytes(img_in, irecv)
        img = jnp.concatenate(by_row(img_in, NORB // 2), axis=1)
        proj = lax.dot_general(img, filt_mat[...], contract, preferred_element_type=jnp.float32)
        for j in range(NBAND // 2):
            target = band_at(j // 8, lax.rem(y + 6 + (j // 2) % 4, 8), j % 2)
            rows_out[target, 1] = proj[2 * j:2 * j + 2]

        def body(i, _):
            step = image_step(i // 8)
            x_ = lax.rem(x + 2 + (i // 2) % 4, 4)
            target = band_at(x_, lax.rem(y + 8 - step, 8), lax.rem(zl + 1 + i, 2))
            send_or_keep(rows_out.at[target], rows_in.at[my_chunk], target, rsend, rrecv)
            return 0

        lax.fori_loop(0, NBAND // 2, body, 0)

    all_bytes(rows_in, rrecv)
    sums[dom] = jnp.sum(rows_in[...], axis=0)

    def to_dom(i, _):
        zh_ = lax.rem(dom // 2 + 2 + i // 2, 4)
        pltpu.make_async_remote_copy(
            src_ref=sums.at[dom], dst_ref=sums.at[dom], send_sem=dsend, recv_sem=drecv,
            device_id=(band, zh_ * 2 + lax.rem(dom + 1 + i, 2)), device_id_type=MESH).start()
        return 0

    lax.fori_loop(0, 4, to_dom, 0)
    lax.fori_loop(6, 8, to_dom, 0)
    pltpu.make_async_remote_copy(
        src_ref=sums.at[dom], dst_ref=sums.at[dom], send_sem=dsend, recv_sem=drecv,
        device_id=(band, dom + 1 - 2 * (dom % 2)), device_id_type=MESH).start()
    others = sums.at[pl.ds(0, NDOM - 1)]
    all_bytes(others, drecv)
    cell_scale = 1.0 / (PLANES * ROWS * LANES * NDOM)
    out_ref[...] = jnp.sum(sums[...], axis=0) * cell_scale

    for s in range(4):
        for o in range(2):
            halo_sent(s, o)

    @pl.when(owner)
    def _():
        all_bytes(filt_in.at[pl.ds(0, 47)], fsend)
        all_bytes(rows_out.at[pl.ds(0, NBAND // 2 - 1)], rsend)

    @pl.when(jnp.logical_not(owner))
    def _():
        all_bytes(filt_in.at[pl.ds(0, 48)], fsend)
        all_bytes(img_out, isend)

    @pl.when(owner)
    def _():
        all_bytes(img_out.at[pl.ds(0, CHUNKS - 1)], isend)

    all_bytes(others, dsend)


def per_device(orbitals, potential):
    bf16, f32 = jnp.bfloat16, jnp.float32
    dma = pltpu.SemaphoreType.DMA
    out = pl.pallas_call(
        kernel,
        out_shape=jax.ShapeDtypeStruct((2, 2, LANES), f32),
        in_specs=[pl.BlockSpec(memory_space=pltpu.HBM)] * 2,
        out_specs=pl.BlockSpec(memory_space=pltpu.VMEM),
        scratch_shapes=[
            pltpu.VMEM((4, 2, PLANES, ROWS, LANES), bf16),
            pltpu.VMEM((PLANES, ROWS, LANES), f32),
            pltpu.VMEM((4, 2, 2, PLANES, ROWS, LANES), bf16),
            pltpu.VMEM((4, 2, PLANES, ROWS, LANES), f32),
            pltpu.VMEM((2, PLANES, ROWS, LANES), f32),
            pltpu.VMEM((CHUNKS, 2, 8, LANES), bf16),
            pltpu.VMEM((CHUNKS, 2, 8, LANES), bf16),
            pltpu.VMEM((NBAND, 2, 8, LANES), bf16),
            pltpu.VMEM((NBAND // 2, 2, 8, LANES), bf16),
            pltpu.VMEM((NORB * 8, LANES), f32),
            pltpu.VMEM((NORB, 8 * LANES), bf16),
            pltpu.VMEM((NBAND, 2, 2, LANES), f32),
            pltpu.VMEM((CHUNKS, 2, 2, LANES), f32),
            pltpu.VMEM((NDOM, 2, 2, LANES), f32),
            dma((2,)), dma((4, 2, 2)), dma((4, 2, 2)),
            dma, dma, dma, dma, dma, dma, dma, dma,
        ],
        compiler_params=pltpu.CompilerParams(collective_id=0, has_side_effects=True, vmem_limit_bytes=40 << 20),
    )(orbitals, potential)
    return out[0], out[1]


def solution(mesh):
    placed = (P("band", "dom", None, None), P("dom", None, None))
    return jax.shard_map(
        per_device,
        mesh=mesh,
        in_specs=placed,
        out_specs=(P("band", None), P("band", None)),
        check_vma=False,
    )
```

```python
import jax
import jax.numpy as jnp
from jax import lax
from jax.experimental import pallas as pl
from jax.experimental.pallas import tpu as pltpu
from jax.sharding import PartitionSpec as P

STENCIL = (
    -5369.0 / 1800.0,
    12.0 / 7.0,
    -15.0 / 56.0,
    10.0 / 189.0,
    -1.0 / 112.0,
    2.0 / 1925.0,
    -1.0 / 16632.0,
)
HALF = tuple(-0.5 * w for w in STENCIL)
CENTER = 8.5
SCALE = 1.0 / 5.5
MESH = pl.DeviceIdType.MESH
NBAND, NDOM = 64, 8
PLANES, ROWS, LANES = 6, 32, 128
CHUNKS = 24
NORB = 128


def image_step(t):
    return lax.rem(10 - t, 8)


def device_at(x, y, z, core):
    return (x * 8 + y) * 2 + z % 2, z // 2 * 2 + core


def kernel(
    orb_hbm, pot_hbm, out_ref,
    slab, pot, halo, fields, acc, filt_out, img_out, filt_in, img_in, wide, filt_mat, rows_out, rows_in, my_sum, sums,
    own_send, own_recv, pot_send, pot_recv, hsend, hrecv, fsend, frecv, isend, irecv, rsend, rrecv, dsend, drecv,
):
    band = lax.axis_index("band")
    dom = lax.axis_index("dom")
    x, y, zl, core = band // 16, (band // 2) % 8, band % 2, dom % 2
    z = dom // 2 * 2 + zl
    role = x * 16 + y * 2 + core
    same = zl == core
    place = x * 2 + core
    owner = jnp.logical_and(place != 0, place != 5)
    my_chunk = (place - 1 - place // 6) * 4 + y % 4

    barrier = pltpu.get_barrier_semaphore()

    def greet(device):
        pl.semaphore_signal(barrier, inc=1, device_id=device, device_id_type=MESH)

    def greet_column(k, _):
        other = lax.rem(z * 2 + core + k, 16)
        greet(device_at(x, y, other // 2, other % 2))
        return 0

    def greet_plane(k, _):
        other = lax.rem(x * 8 + y + k // 2, 32)
        greet(device_at(other // 8, other % 8, z, k % 2))
        return 0

    lax.fori_loop(1, 16, greet_column, 0)
    lax.fori_loop(2, 64, greet_plane, 0)

    def load(o):
        return pltpu.make_async_copy(orb_hbm.at[o], slab.at[0, o], own_recv.at[o])

    def move(o):
        return pltpu.make_async_remote_copy(
            src_ref=orb_hbm.at[o], dst_ref=slab.at[0, o], send_sem=own_send.at[o], recv_sem=own_recv.at[o],
            device_id=device_at(x, y, dom, zl), device_id_type=MESH)

    load_pot = pltpu.make_async_copy(pot_hbm, pot, pot_recv)
    share_pot = pltpu.make_async_remote_copy(
        src_ref=pot_hbm, dst_ref=pot, send_sem=pot_send, recv_sem=pot_recv,
        device_id=(band, dom + 1 - 2 * core), device_id_type=MESH)

    @pl.when(same)
    def _():
        load(0).start()
        load(1).start()
        load_pot.start()

    @pl.when(z == 0)
    def _():
        for s in range(4):
            halo[s, 0] = jnp.zeros((2, PLANES, ROWS, LANES), jnp.bfloat16)

    @pl.when(z == NDOM - 1)
    def _():
        for s in range(4):
            halo[s, 1] = jnp.zeros((2, PLANES, ROWS, LANES), jnp.bfloat16)

    def local_part(s, shift):
        def body(o, _):
            for p in range(PLANES):
                v = fields[s, o, p]
                total = (pot[p] + (3.0 * HALF[0] + shift)) * v
                for k in range(1, 7):
                    along_y = pltpu.roll(v, k, 0) + pltpu.roll(v, ROWS - k, 0)
                    along_x = pltpu.roll(v, k, 1) + pltpu.roll(v, LANES - k, 1)
                    total = total + HALF[k] * (along_y + along_x)
                for q in range(PLANES):
                    if q != p:
                        total = total + HALF[abs(p - q)] * fields[s, o, q]
                acc[o, p] = total
            return 0

        lax.fori_loop(0, 2, body, 0)

    def halo_copies(s, o, h):
        rows = pl.ds(16 * h, 16)
        if s == 0:
            source, at, core_ = orb_hbm.at[o, :, rows, :], dom, zl
        else:
            source, at, core_ = slab.at[s, o, :, rows, :], z, core
        return at, [
            pltpu.make_async_remote_copy(
                src_ref=source, dst_ref=halo.at[s, side, o, :, rows, :],
                send_sem=hsend.at[s, side, o, h], recv_sem=hrecv.at[s, side, o, h],
                device_id=device_at(x, y, lax.rem(at + step, 8), core_), device_id_type=MESH)
            for side, step in ((0, 1), (1, 7))
        ]

    def halo_start(s, o, h):
        at, (up, down) = halo_copies(s, o, h)

        @pl.when(at < NDOM - 1)
        def _():
            up.start()

        @pl.when(at > 0)
        def _():
            down.start()

    def halo_wait(s, o, h):
        _, (up, down) = halo_copies(s, o, h)

        @pl.when(z > 0)
        def _():
            up.wait_recv()

        @pl.when(z < NDOM - 1)
        def _():
            down.wait_recv()

    def halo_sent(s, o, h):
        at, (up, down) = halo_copies(s, o, h)

        @pl.when(at < NDOM - 1)
        def _():
            up.wait_send()

        @pl.when(at > 0)
        def _():
            down.wait_send()

    def halo_part(s, o, h, store):
        rows = pl.ds(16 * h, 16)
        low = [halo[s, 0, o, j, rows, :].astype(jnp.float32) for j in range(PLANES)]
        high = [halo[s, 1, o, j, rows, :].astype(jnp.float32) for j in range(PLANES)]
        for p in range(PLANES):
            total = acc[o, p, rows, :]
            for j in range(p, PLANES):
                total = total + HALF[p + 6 - j] * low[j]
            for j in range(p + 1):
                total = total + HALF[6 + j - p] * high[j]
            store(o, p, h, rows, total)

    def store_field(s):
        def store(o, p, h, rows, total):
            if s == 1:
                value = SCALE * total
            else:
                value = (2.0 * SCALE) * total - fields[s - 2, o, p, rows, :]
            fields[s, o, p, rows, :] = value
            slab[s, o, p, rows, :] = value.astype(jnp.bfloat16)
            if s == 3:
                for t in range(2):
                    filt_out[p * 4 + h * 2 + t, o] = value[8 * t:8 * t + 8].astype(jnp.bfloat16)

        return store

    def store_image(o, p, h, rows, total):
        for t in range(2):
            img_out[p * 4 + h * 2 + t, o] = total[8 * t:8 * t + 8].astype(jnp.bfloat16)

    def send_or_keep(src, dst, target, send_sem, recv_sem):
        x_, y_, core_ = target
        here = jnp.logical_and(y_ == y, x_ * 2 + core_ == place)

        @pl.when(here)
        def _():
            pltpu.make_async_copy(src, dst, recv_sem).start()

        @pl.when(jnp.logical_not(here))
        def _():
            pltpu.make_async_remote_copy(
                src_ref=src, dst_ref=dst, send_sem=send_sem, recv_sem=recv_sem,
                device_id=device_at(x_, y_, z, core_), device_id_type=MESH).start()

    def to_owners(src, dst, slot_of, step_of, steps, send_sem, recv_sem):
        def body(i, _):
            step = step_of(i // 6)
            r = i % 6
            place_ = r + 1 + r // 4
            y_ = lax.rem(y + step, 8)
            send_or_keep(src.at[r * 4 + y_ % 4], dst.at[slot_of(step)], (place_ // 2, y_, place_ % 2), send_sem, recv_sem)
            return 0

        lax.fori_loop(0, 6 * steps, body, 0)

    def all_bytes(ref, sem):
        pltpu.make_async_copy(ref, ref, sem).wait()

    pieces = [(o, h) for o in range(2) for h in range(2)]
    pl.semaphore_wait(barrier, 77)

    @pl.when(same)
    def _():
        share_pot.start()

    @pl.when(jnp.logical_not(same))
    def _():
        move(0).start()
        move(1).start()

    for o, h in pieces:
        halo_start(0, o, h)
    for o in range(2):
        load(o).wait()
    load_pot.wait()

    def widen(o, _):
        fields[0, o] = slab[0, o].astype(jnp.float32)
        return 0

    lax.fori_loop(0, 2, widen, 0)
    local_part(0, -CENTER)
    for s in range(3):
        for o, h in pieces:
            halo_wait(s, o, h)
            halo_part(s, o, h, store_field(s + 1))
            halo_start(s + 1, o, h)
        if s == 2:
            to_owners(filt_out, filt_in, lambda step: role, lambda t: 4 + ((t + 1) // 2) * (1 - 2 * (t % 2)), 8, fsend, frecv)
        local_part(s + 1, -CENTER if s < 2 else 0.0)
    for o, h in pieces:
        halo_wait(3, o, h)
        halo_part(3, o, h, store_image)
    to_owners(img_out, img_in, lambda step: x * 8 + lax.rem(10 - step, 8) * 2 + core, image_step, 4, isend, irecv)

    def by_row(src, count):
        rows = wide.at[pl.ds(0, count * 8)]
        rows[...] = src[...].astype(jnp.float32).reshape(count * 8, LANES)
        return [wide[pl.ds(r, count, stride=8), :].astype(jnp.bfloat16) for r in range(8)]

    contract = (((1,), (1,)), ((), ()))

    @pl.when(owner)
    def _():
        all_bytes(filt_in, frecv)
        filt = by_row(filt_in, NORB)
        for r in range(8):
            filt_mat[:, r * LANES:(r + 1) * LANES] = filt[r]
        mat = filt_mat[...]
        corr = lax.dot_general(mat, mat, contract, preferred_element_type=jnp.float32)
        for b in range(NBAND):
            rows_out[b, 0] = corr[2 * b:2 * b + 2]
        all_bytes(img_in, irecv)
        img = jnp.concatenate(by_row(img_in, NORB // 2), axis=1)
        proj = lax.dot_general(img, filt_mat[...], contract, preferred_element_type=jnp.float32)
        for j in range(NBAND // 2):
            target = j // 8 * 16 + lax.rem(y + 6 + (j // 2) % 4, 8) * 2 + j % 2
            rows_out[target, 1] = proj[2 * j:2 * j + 2]

        def body(i, _):
            step = image_step(i // 8)
            x_, y_, core_ = lax.rem(x + 2 + (i // 2) % 4, 4), lax.rem(y + 8 - step, 8), lax.rem(core + 1 + i, 2)
            target = x_ * 16 + y_ * 2 + core_
            send_or_keep(rows_out.at[target], rows_in.at[my_chunk], (x_, y_, core_), rsend, rrecv)
            return 0

        lax.fori_loop(0, NBAND // 2, body, 0)

    all_bytes(rows_in, rrecv)
    my_sum[...] = jnp.sum(rows_in[...], axis=0)

    def to_dom(i, _):
        dom_ = lax.rem(dom // 2 * 2 + 4 + i, 8)
        here = jnp.logical_and(same, dom_ == dom)

        @pl.when(here)
        def _():
            pltpu.make_async_copy(my_sum, sums.at[z], drecv).start()

        @pl.when(jnp.logical_not(here))
        def _():
            pltpu.make_async_remote_copy(
                src_ref=my_sum, dst_ref=sums.at[z], send_sem=dsend, recv_sem=drecv,
                device_id=(role, dom_), device_id_type=MESH).start()

        return 0

    lax.fori_loop(0, NDOM, to_dom, 0)
    all_bytes(sums, drecv)
    cell_scale = 1.0 / (PLANES * ROWS * LANES * NDOM)
    out_ref[...] = jnp.sum(sums[...], axis=0) * cell_scale

    for s in range(4):
        for o, h in pieces:
            halo_sent(s, o, h)

    @pl.when(same)
    def _():
        share_pot.wait_send()
        all_bytes(sums.at[pl.ds(0, NDOM - 1)], dsend)

    @pl.when(jnp.logical_not(same))
    def _():
        move(0).wait_send()
        move(1).wait_send()
        all_bytes(sums, dsend)

    @pl.when(owner)
    def _():
        all_bytes(filt_in.at[pl.ds(0, 47)], fsend)
        all_bytes(img_out.at[pl.ds(0, CHUNKS - 1)], isend)
        all_bytes(rows_out.at[pl.ds(0, NBAND // 2 - 1)], rsend)

    @pl.when(jnp.logical_not(owner))
    def _():
        all_bytes(filt_in.at[pl.ds(0, 48)], fsend)
        all_bytes(img_out, isend)


def per_device(orbitals, potential):
    bf16, f32 = jnp.bfloat16, jnp.float32
    dma = pltpu.SemaphoreType.DMA
    out = pl.pallas_call(
        kernel,
        out_shape=jax.ShapeDtypeStruct((2, 2, LANES), f32),
        in_specs=[pl.BlockSpec(memory_space=pltpu.HBM)] * 2,
        out_specs=pl.BlockSpec(memory_space=pltpu.VMEM),
        scratch_shapes=[
            pltpu.VMEM((4, 2, PLANES, ROWS, LANES), bf16),
            pltpu.VMEM((PLANES, ROWS, LANES), f32),
            pltpu.VMEM((4, 2, 2, PLANES, ROWS, LANES), bf16),
            pltpu.VMEM((4, 2, PLANES, ROWS, LANES), f32),
            pltpu.VMEM((2, PLANES, ROWS, LANES), f32),
            pltpu.VMEM((CHUNKS, 2, 8, LANES), bf16),
            pltpu.VMEM((CHUNKS, 2, 8, LANES), bf16),
            pltpu.VMEM((NBAND, 2, 8, LANES), bf16),
            pltpu.VMEM((NBAND // 2, 2, 8, LANES), bf16),
            pltpu.VMEM((NORB * 8, LANES), f32),
            pltpu.VMEM((NORB, 8 * LANES), bf16),
            pltpu.VMEM((NBAND, 2, 2, LANES), f32),
            pltpu.VMEM((CHUNKS, 2, 2, LANES), f32),
            pltpu.VMEM((2, 2, LANES), f32),
            pltpu.VMEM((NDOM, 2, 2, LANES), f32),
            dma((2,)), dma((2,)), dma, dma, dma((4, 2, 2, 2)), dma((4, 2, 2, 2)),
            dma, dma, dma, dma, dma, dma, dma, dma,
        ],
        compiler_params=pltpu.CompilerParams(collective_id=0, has_side_effects=True, vmem_limit_bytes=(64 << 20) - (64 << 10)),
    )(orbitals, potential)
    return out[0], out[1]


def solution(mesh):
    placed = (P("band", "dom", None, None), P("dom", None, None))
    return jax.shard_map(
        per_device,
        mesh=mesh,
        in_specs=placed,
        out_specs=(P("band", None), P("band", None)),
        check_vma=False,
    )
```

```python
import jax
import jax.numpy as jnp
from jax import lax
from jax.experimental import pallas as pl
from jax.experimental.pallas import tpu as pltpu
from jax.sharding import PartitionSpec as P

STENCIL = (
    -5369.0 / 1800.0,
    12.0 / 7.0,
    -15.0 / 56.0,
    10.0 / 189.0,
    -1.0 / 112.0,
    2.0 / 1925.0,
    -1.0 / 16632.0,
)
HALF = tuple(-0.5 * w for w in STENCIL)
CENTER = 8.5
SCALE = 1.0 / 5.5
MESH = pl.DeviceIdType.MESH
NBAND, NDOM = 64, 8
PLANES, ROWS, LANES = 6, 32, 128
CHUNKS = 24
NORB = 128


def image_step(t):
    return lax.rem(10 - t, 8)


def device_at(x, y, z, core):
    return (x * 8 + y) * 2 + z % 2, z // 2 * 2 + core


def kernel(
    orb_hbm, pot_hbm, out_ref,
    slab, pot, halo, fields, acc, filt_out, img_out, filt_in, img_in, wide, filt_mat, rows_out, rows_in, my_sum, sums,
    relay_sem, own_send, own_recv, pot_send, pot_recv, hsend, hrecv, fsend, frecv, isend, irecv, rsend, rrecv, dsend, drecv,
):
    band = lax.axis_index("band")
    dom = lax.axis_index("dom")
    x, y, zl, core = band // 16, (band // 2) % 8, band % 2, dom % 2
    z = dom // 2 * 2 + zl
    role = x * 16 + y * 2 + core
    same = zl == core
    place = x * 2 + core
    owner = jnp.logical_and(place != 0, place != 5)
    my_chunk = (place - 1 - place // 6) * 4 + y % 4

    def greet(sem, x_, y_, z_, core_):
        pl.semaphore_signal(sem, inc=1, device_id=device_at(lax.rem(x_, 4), lax.rem(y_, 8), lax.rem(z_, 8), core_), device_id_type=MESH)

    barrier = pltpu.get_barrier_semaphore()
    for step in (2, 6, 1, 7):
        for core_ in range(2):
            greet(barrier, x, y, z + step, core_)
    greet(barrier, x, y, z, 1 - core)
    for step in (2, 6, 1, 7):
        greet(barrier, x, y + step, z, core)
    for step in (2, 1, 3):
        greet(barrier, x + step, y, z, core)

    def relay(stage):
        if stage == 0:
            for step in (2, 6):
                greet(relay_sem.at[0], x, y + step, z, core)
                greet(relay_sem.at[0], x, y, z + step, core)
        elif stage == 1:
            pl.semaphore_wait(relay_sem.at[0], 4)
            for step in (2, 1, 3):
                greet(relay_sem.at[1], x + step, y, z, core)
        elif stage == 2:
            pl.semaphore_wait(relay_sem.at[1], 3)
            greet(relay_sem.at[2], x, y, z, 1 - core)
        else:
            pl.semaphore_wait(relay_sem.at[2], 1)

    def load(o):
        return pltpu.make_async_copy(orb_hbm.at[o], slab.at[0, o], own_recv.at[o])

    def move(o):
        return pltpu.make_async_remote_copy(
            src_ref=orb_hbm.at[o], dst_ref=slab.at[0, o], send_sem=own_send.at[o], recv_sem=own_recv.at[o],
            device_id=device_at(x, y, dom, zl), device_id_type=MESH)

    load_pot = pltpu.make_async_copy(pot_hbm, pot, pot_recv)
    share_pot = pltpu.make_async_remote_copy(
        src_ref=pot_hbm, dst_ref=pot, send_sem=pot_send, recv_sem=pot_recv,
        device_id=(band, dom + 1 - 2 * core), device_id_type=MESH)

    @pl.when(same)
    def _():
        load(0).start()
        load(1).start()
        load_pot.start()

    @pl.when(z == 0)
    def _():
        for s in range(4):
            halo[s, 0] = jnp.zeros((2, PLANES, ROWS, LANES), jnp.bfloat16)

    @pl.when(z == NDOM - 1)
    def _():
        for s in range(4):
            halo[s, 1] = jnp.zeros((2, PLANES, ROWS, LANES), jnp.bfloat16)

    def local_part(s, shift):
        def body(o, _):
            for p in range(PLANES):
                v = fields[s, o, p]
                total = (pot[p] + (3.0 * HALF[0] + shift)) * v
                for k in range(1, 7):
                    along_y = pltpu.roll(v, k, 0) + pltpu.roll(v, ROWS - k, 0)
                    along_x = pltpu.roll(v, k, 1) + pltpu.roll(v, LANES - k, 1)
                    total = total + HALF[k] * (along_y + along_x)
                for q in range(PLANES):
                    if q != p:
                        total = total + HALF[abs(p - q)] * fields[s, o, q]
                acc[o, p] = total
            return 0

        lax.fori_loop(0, 2, body, 0)

    def halo_copies(s, o, h):
        rows = pl.ds(16 * h, 16)
        if s == 0:
            source, at, core_ = orb_hbm.at[o, :, rows, :], dom, zl
        else:
            source, at, core_ = slab.at[s, o, :, rows, :], z, core
        return at, [
            pltpu.make_async_remote_copy(
                src_ref=source, dst_ref=halo.at[s, side, o, :, rows, :],
                send_sem=hsend.at[s, side, o, h], recv_sem=hrecv.at[s, side, o, h],
                device_id=device_at(x, y, lax.rem(at + step, 8), core_), device_id_type=MESH)
            for side, step in ((0, 1), (1, 7))
        ]

    def halo_start(s, o, h):
        at, (up, down) = halo_copies(s, o, h)

        @pl.when(at < NDOM - 1)
        def _():
            up.start()

        @pl.when(at > 0)
        def _():
            down.start()

    def halo_wait(s, o, h):
        _, (up, down) = halo_copies(s, o, h)

        @pl.when(z > 0)
        def _():
            up.wait_recv()

        @pl.when(z < NDOM - 1)
        def _():
            down.wait_recv()

    def halo_sent(s, o, h):
        at, (up, down) = halo_copies(s, o, h)

        @pl.when(at < NDOM - 1)
        def _():
            up.wait_send()

        @pl.when(at > 0)
        def _():
            down.wait_send()

    def halo_part(s, o, h, store):
        rows = pl.ds(16 * h, 16)
        low = [halo[s, 0, o, j, rows, :].astype(jnp.float32) for j in range(PLANES)]
        high = [halo[s, 1, o, j, rows, :].astype(jnp.float32) for j in range(PLANES)]
        for p in range(PLANES):
            total = acc[o, p, rows, :]
            for j in range(p, PLANES):
                total = total + HALF[p + 6 - j] * low[j]
            for j in range(p + 1):
                total = total + HALF[6 + j - p] * high[j]
            store(o, p, h, rows, total)

    def store_field(s):
        def store(o, p, h, rows, total):
            if s == 1:
                value = SCALE * total
            else:
                value = (2.0 * SCALE) * total - fields[s - 2, o, p, rows, :]
            fields[s, o, p, rows, :] = value
            slab[s, o, p, rows, :] = value.astype(jnp.bfloat16)
            if s == 3:
                for t in range(2):
                    filt_out[p * 4 + h * 2 + t, o] = value[8 * t:8 * t + 8].astype(jnp.bfloat16)

        return store

    def store_image(o, p, h, rows, total):
        for t in range(2):
            img_out[p * 4 + h * 2 + t, o] = total[8 * t:8 * t + 8].astype(jnp.bfloat16)

    def send_or_keep(src, dst, target, send_sem, recv_sem):
        x_, y_, core_ = target
        here = jnp.logical_and(y_ == y, x_ * 2 + core_ == place)

        @pl.when(here)
        def _():
            pltpu.make_async_copy(src, dst, recv_sem).start()

        @pl.when(jnp.logical_not(here))
        def _():
            pltpu.make_async_remote_copy(
                src_ref=src, dst_ref=dst, send_sem=send_sem, recv_sem=recv_sem,
                device_id=device_at(x_, y_, z, core_), device_id_type=MESH).start()

    def to_owners(src, dst, slot_of, step_of, steps, send_sem, recv_sem):
        def body(i, _):
            step = step_of(i // 6)
            r = i % 6
            place_ = r + 1 + r // 4
            y_ = lax.rem(y + step, 8)
            send_or_keep(src.at[r * 4 + y_ % 4], dst.at[slot_of(step)], (place_ // 2, y_, place_ % 2), send_sem, recv_sem)
            return 0

        lax.fori_loop(0, 6 * steps, body, 0)

    def all_bytes(ref, sem):
        pltpu.make_async_copy(ref, ref, sem).wait()

    pieces = [(o, h) for o in range(2) for h in range(2)]
    pl.semaphore_wait(barrier, 16)

    @pl.when(same)
    def _():
        share_pot.start()

    @pl.when(jnp.logical_not(same))
    def _():
        move(0).start()
        move(1).start()

    for o, h in pieces:
        halo_start(0, o, h)
    relay(0)
    for o in range(2):
        load(o).wait()
    load_pot.wait()

    def widen(o, _):
        fields[0, o] = slab[0, o].astype(jnp.float32)
        return 0

    lax.fori_loop(0, 2, widen, 0)
    local_part(0, -CENTER)
    relay(1)
    for s in range(3):
        for o, h in pieces:
            halo_wait(s, o, h)
            halo_part(s, o, h, store_field(s + 1))
            halo_start(s + 1, o, h)
        if s == 2:
            to_owners(filt_out, filt_in, lambda step: role, lambda t: 4 + ((t + 1) // 2) * (1 - 2 * (t % 2)), 8, fsend, frecv)
        local_part(s + 1, -CENTER if s < 2 else 0.0)
        if s < 2:
            relay(s + 2)
    for o, h in pieces:
        halo_wait(3, o, h)
        halo_part(3, o, h, store_image)
    to_owners(img_out, img_in, lambda step: x * 8 + lax.rem(10 - step, 8) * 2 + core, image_step, 4, isend, irecv)

    def by_row(src, count):
        rows = wide.at[pl.ds(0, count * 8)]
        rows[...] = src[...].astype(jnp.float32).reshape(count * 8, LANES)
        return [wide[pl.ds(r, count, stride=8), :].astype(jnp.bfloat16) for r in range(8)]

    contract = (((1,), (1,)), ((), ()))

    @pl.when(owner)
    def _():
        all_bytes(filt_in, frecv)
        filt = by_row(filt_in, NORB)
        for r in range(8):
            filt_mat[:, r * LANES:(r + 1) * LANES] = filt[r]
        mat = filt_mat[...]
        corr = lax.dot_general(mat, mat, contract, preferred_element_type=jnp.float32)
        for b in range(NBAND):
            rows_out[b, 0] = corr[2 * b:2 * b + 2]
        all_bytes(img_in, irecv)
        img = jnp.concatenate(by_row(img_in, NORB // 2), axis=1)
        proj = lax.dot_general(img, filt_mat[...], contract, preferred_element_type=jnp.float32)
        for j in range(NBAND // 2):
            target = j // 8 * 16 + lax.rem(y + 6 + (j // 2) % 4, 8) * 2 + j % 2
            rows_out[target, 1] = proj[2 * j:2 * j + 2]

        def body(i, _):
            step = image_step(i // 8)
            x_, y_, core_ = lax.rem(x + 2 + (i // 2) % 4, 4), lax.rem(y + 8 - step, 8), lax.rem(core + 1 + i, 2)
            target = x_ * 16 + y_ * 2 + core_
            send_or_keep(rows_out.at[target], rows_in.at[my_chunk], (x_, y_, core_), rsend, rrecv)
            return 0

        lax.fori_loop(0, NBAND // 2, body, 0)

    all_bytes(rows_in, rrecv)
    my_sum[...] = jnp.sum(rows_in[...], axis=0)

    def to_dom(i, _):
        dom_ = lax.rem(dom // 2 * 2 + 4 + i, 8)
        here = jnp.logical_and(same, dom_ == dom)

        @pl.when(here)
        def _():
            pltpu.make_async_copy(my_sum, sums.at[z], drecv).start()

        @pl.when(jnp.logical_not(here))
        def _():
            pltpu.make_async_remote_copy(
                src_ref=my_sum, dst_ref=sums.at[z], send_sem=dsend, recv_sem=drecv,
                device_id=(role, dom_), device_id_type=MESH).start()

        return 0

    lax.fori_loop(0, NDOM, to_dom, 0)
    all_bytes(sums, drecv)
    cell_scale = 1.0 / (PLANES * ROWS * LANES * NDOM)
    out_ref[...] = jnp.sum(sums[...], axis=0) * cell_scale

    for s in range(4):
        for o, h in pieces:
            halo_sent(s, o, h)

    @pl.when(same)
    def _():
        share_pot.wait_send()
        all_bytes(sums.at[pl.ds(0, NDOM - 1)], dsend)

    @pl.when(jnp.logical_not(same))
    def _():
        move(0).wait_send()
        move(1).wait_send()
        all_bytes(sums, dsend)

    @pl.when(owner)
    def _():
        all_bytes(filt_in.at[pl.ds(0, 47)], fsend)
        all_bytes(img_out.at[pl.ds(0, CHUNKS - 1)], isend)
        all_bytes(rows_out.at[pl.ds(0, NBAND // 2 - 1)], rsend)

    @pl.when(jnp.logical_not(owner))
    def _():
        all_bytes(filt_in.at[pl.ds(0, 48)], fsend)
        all_bytes(img_out, isend)


def per_device(orbitals, potential):
    bf16, f32 = jnp.bfloat16, jnp.float32
    dma = pltpu.SemaphoreType.DMA
    out = pl.pallas_call(
        kernel,
        out_shape=jax.ShapeDtypeStruct((2, 2, LANES), f32),
        in_specs=[pl.BlockSpec(memory_space=pltpu.HBM)] * 2,
        out_specs=pl.BlockSpec(memory_space=pltpu.VMEM),
        scratch_shapes=[
            pltpu.VMEM((4, 2, PLANES, ROWS, LANES), bf16),
            pltpu.VMEM((PLANES, ROWS, LANES), f32),
            pltpu.VMEM((4, 2, 2, PLANES, ROWS, LANES), bf16),
            pltpu.VMEM((4, 2, PLANES, ROWS, LANES), f32),
            pltpu.VMEM((2, PLANES, ROWS, LANES), f32),
            pltpu.VMEM((CHUNKS, 2, 8, LANES), bf16),
            pltpu.VMEM((CHUNKS, 2, 8, LANES), bf16),
            pltpu.VMEM((NBAND, 2, 8, LANES), bf16),
            pltpu.VMEM((NBAND // 2, 2, 8, LANES), bf16),
            pltpu.VMEM((NORB * 8, LANES), f32),
            pltpu.VMEM((NORB, 8 * LANES), bf16),
            pltpu.VMEM((NBAND, 2, 2, LANES), f32),
            pltpu.VMEM((CHUNKS, 2, 2, LANES), f32),
            pltpu.VMEM((2, 2, LANES), f32),
            pltpu.VMEM((NDOM, 2, 2, LANES), f32),
            pltpu.SemaphoreType.REGULAR((3,)), dma((2,)), dma((2,)), dma, dma, dma((4, 2, 2, 2)), dma((4, 2, 2, 2)),
            dma, dma, dma, dma, dma, dma, dma, dma,
        ],
        compiler_params=pltpu.CompilerParams(collective_id=0, has_side_effects=True, vmem_limit_bytes=(64 << 20) - (64 << 10)),
    )(orbitals, potential)
    return out[0], out[1]


def solution(mesh):
    placed = (P("band", "dom", None, None), P("dom", None, None))
    return jax.shard_map(
        per_device,
        mesh=mesh,
        in_specs=placed,
        out_specs=(P("band", None), P("band", None)),
        check_vma=False,
    )
```

```python
import jax
import jax.numpy as jnp
from jax import lax
from jax.experimental import pallas as pl
from jax.experimental.pallas import tpu as pltpu
from jax.sharding import PartitionSpec as P

STENCIL = (
    -5369.0 / 1800.0,
    12.0 / 7.0,
    -15.0 / 56.0,
    10.0 / 189.0,
    -1.0 / 112.0,
    2.0 / 1925.0,
    -1.0 / 16632.0,
)
HALF = tuple(-0.5 * w for w in STENCIL)
CENTER = 8.5
SCALE = 1.0 / 5.5
MESH = pl.DeviceIdType.MESH
NBAND, NDOM = 64, 8
PLANES, ROWS, LANES = 6, 32, 128
CHUNKS = 24
NORB = 128


def image_step(t):
    return lax.rem(10 - t, 8)


def device_at(x, y, z, core):
    return (x * 8 + y) * 2 + z % 2, z // 2 * 2 + core


def kernel(
    orb_hbm, pot_hbm, out_ref,
    slab, pot, halo, fields, acc, filt_out, img_out, filt_in, img_in, wide, filt_mat, rows_out, rows_in, my_sum, sums,
    relay_sem, own_send, own_recv, pot_send, pot_recv, hsend, hrecv, fsend, frecv, isend, irecv, rsend, rrecv, dsend, drecv,
):
    band = lax.axis_index("band")
    dom = lax.axis_index("dom")
    x, y, zl, core = band // 16, (band // 2) % 8, band % 2, dom % 2
    z = dom // 2 * 2 + zl
    role = x * 16 + y * 2 + core
    same = zl == core
    place = x * 2 + core
    owner = jnp.logical_and(place != 0, place != 5)
    my_chunk = (place - 1 - place // 6) * 4 + y % 4

    def greet(sem, x_, y_, z_, core_):
        pl.semaphore_signal(sem, inc=1, device_id=device_at(lax.rem(x_, 4), lax.rem(y_, 8), lax.rem(z_, 8), core_), device_id_type=MESH)

    barrier = pltpu.get_barrier_semaphore()
    for step in (2, 6, 1, 7):
        for core_ in range(2):
            greet(barrier, x, y, z + step, core_)
    greet(barrier, x, y, z, 1 - core)
    for step in (2, 6, 1, 7):
        greet(barrier, x, y + step, z, core)
    for step in (2, 1, 3):
        greet(barrier, x + step, y, z, core)

    def relay(stage):
        if stage == 0:
            for step in (2, 6):
                greet(relay_sem.at[0], x, y + step, z, core)
                greet(relay_sem.at[0], x, y, z + step, core)
        elif stage == 1:
            pl.semaphore_wait(relay_sem.at[0], 4)
            for step in (2, 1, 3):
                greet(relay_sem.at[1], x + step, y, z, core)
        elif stage == 2:
            pl.semaphore_wait(relay_sem.at[1], 3)
            greet(relay_sem.at[2], x, y, z, 1 - core)
        else:
            pl.semaphore_wait(relay_sem.at[2], 1)

    def load(o):
        return pltpu.make_async_copy(orb_hbm.at[o], slab.at[0, o], own_recv.at[o])

    def move(o):
        return pltpu.make_async_remote_copy(
            src_ref=orb_hbm.at[o], dst_ref=slab.at[0, o], send_sem=own_send.at[o], recv_sem=own_recv.at[o],
            device_id=device_at(x, y, dom, zl), device_id_type=MESH)

    load_pot = pltpu.make_async_copy(pot_hbm, pot, pot_recv)
    share_pot = pltpu.make_async_remote_copy(
        src_ref=pot_hbm, dst_ref=pot, send_sem=pot_send, recv_sem=pot_recv,
        device_id=(band, dom + 1 - 2 * core), device_id_type=MESH)

    @pl.when(same)
    def _():
        load(0).start()
        load(1).start()
        load_pot.start()

    @pl.when(z == 0)
    def _():
        for s in range(4):
            halo[s, 0] = jnp.zeros((2, PLANES, ROWS, LANES), jnp.bfloat16)

    @pl.when(z == NDOM - 1)
    def _():
        for s in range(4):
            halo[s, 1] = jnp.zeros((2, PLANES, ROWS, LANES), jnp.bfloat16)

    def local_part(s, o):
        shift = -CENTER if s < 3 else 0.0

        def body(o, _):
            for p in range(PLANES):
                v = fields[s, o, p]
                total = (pot[p] + (3.0 * HALF[0] + shift)) * v
                for k in range(1, 7):
                    along_y = pltpu.roll(v, k, 0) + pltpu.roll(v, ROWS - k, 0)
                    along_x = pltpu.roll(v, k, 1) + pltpu.roll(v, LANES - k, 1)
                    total = total + HALF[k] * (along_y + along_x)
                for q in range(PLANES):
                    if q != p:
                        total = total + HALF[abs(p - q)] * fields[s, o, q]
                acc[o, p] = total
            return 0

        lax.fori_loop(o, o + 1, body, 0)

    def halo_copies(s, o, h):
        rows = pl.ds(16 * h, 16)
        if s == 0:
            source, at, core_ = orb_hbm.at[o, :, rows, :], dom, zl
        else:
            source, at, core_ = slab.at[s, o, :, rows, :], z, core
        return at, [
            pltpu.make_async_remote_copy(
                src_ref=source, dst_ref=halo.at[s, side, o, :, rows, :],
                send_sem=hsend.at[s, side, o, h], recv_sem=hrecv.at[s, side, o, h],
                device_id=device_at(x, y, lax.rem(at + step, 8), core_), device_id_type=MESH)
            for side, step in ((0, 1), (1, 7))
        ]

    def halo_start(s, o, h):
        at, (up, down) = halo_copies(s, o, h)

        @pl.when(at < NDOM - 1)
        def _():
            up.start()

        @pl.when(at > 0)
        def _():
            down.start()

    def halo_wait(s, o, h):
        _, (up, down) = halo_copies(s, o, h)

        @pl.when(z > 0)
        def _():
            up.wait_recv()

        @pl.when(z < NDOM - 1)
        def _():
            down.wait_recv()

    def halo_sent(s, o, h):
        at, (up, down) = halo_copies(s, o, h)

        @pl.when(at < NDOM - 1)
        def _():
            up.wait_send()

        @pl.when(at > 0)
        def _():
            down.wait_send()

    def halo_part(s, o, h, store):
        rows = pl.ds(16 * h, 16)
        low = [halo[s, 0, o, j, rows, :].astype(jnp.float32) for j in range(PLANES)]
        high = [halo[s, 1, o, j, rows, :].astype(jnp.float32) for j in range(PLANES)]
        for p in range(PLANES):
            total = acc[o, p, rows, :]
            for j in range(p, PLANES):
                total = total + HALF[p + 6 - j] * low[j]
            for j in range(p + 1):
                total = total + HALF[6 + j - p] * high[j]
            store(o, p, h, rows, total)

    def store_field(s):
        def store(o, p, h, rows, total):
            if s == 1:
                value = SCALE * total
            else:
                value = (2.0 * SCALE) * total - fields[s - 2, o, p, rows, :]
            fields[s, o, p, rows, :] = value
            slab[s, o, p, rows, :] = value.astype(jnp.bfloat16)
            if s == 3:
                for t in range(2):
                    filt_out[p * 4 + t * 2 + h, o] = value[8 * t:8 * t + 8].astype(jnp.bfloat16)

        return store

    def store_image(o, p, h, rows, total):
        for t in range(2):
            img_out[p * 4 + t * 2 + h, o] = total[8 * t:8 * t + 8].astype(jnp.bfloat16)

    def send_or_keep(src, dst, target, send_sem, recv_sem):
        x_, y_, core_ = target
        here = jnp.logical_and(y_ == y, x_ * 2 + core_ == place)

        @pl.when(here)
        def _():
            pltpu.make_async_copy(src, dst, recv_sem).start()

        @pl.when(jnp.logical_not(here))
        def _():
            pltpu.make_async_remote_copy(
                src_ref=src, dst_ref=dst, send_sem=send_sem, recv_sem=recv_sem,
                device_id=device_at(x_, y_, z, core_), device_id_type=MESH).start()

    def to_owners(half, src, dst, slot_of, steps, send_sem, recv_sem):
        odd = (y + half) % 2
        for even_step in steps:
            step = lax.rem(even_step + 8 - odd, 8)
            y_ = lax.rem(y + step, 8)

            def body(r, _):
                place_ = r + 1 + r // 4
                send_or_keep(src.at[r * 4 + y_ % 4], dst.at[slot_of(step)], (place_ // 2, y_, place_ % 2), send_sem, recv_sem)
                return 0

            lax.fori_loop(0, 6, body, 0)

    def filt_to_owners(half):
        to_owners(half, filt_out, filt_in, lambda step: role, (4, 2, 6, 0), fsend, frecv)

    def img_to_owners(half):
        to_owners(half, img_out, img_in, lambda step: x * 8 + lax.rem(10 - step, 8) * 2 + core, (2, 0), isend, irecv)

    def all_bytes(ref, sem):
        pltpu.make_async_copy(ref, ref, sem).wait()

    pieces = [(o, h) for h in range(2) for o in range(2)]
    pl.semaphore_wait(barrier, 16)

    @pl.when(same)
    def _():
        share_pot.start()

    @pl.when(jnp.logical_not(same))
    def _():
        move(0).start()
        move(1).start()
        for o, h in pieces:
            halo_start(0, o, h)

    relay(0)
    load_pot.wait()
    for o in range(2):
        load(o).wait()
        fields[0, o] = slab[0, o].astype(jnp.float32)
        local_part(0, o)

    @pl.when(same)
    def _():
        for o, h in pieces:
            halo_start(0, o, h)

    relay(1)
    for s in range(3):
        for o, h in pieces:
            halo_wait(s, o, h)
            halo_part(s, o, h, store_field(s + 1))
            halo_start(s + 1, o, h)
            if s == 2 and o == 1:
                filt_to_owners(h)
        for o in range(2):
            local_part(s + 1, o)
        if s < 2:
            relay(s + 2)
    for o, h in pieces:
        halo_wait(3, o, h)
        halo_part(3, o, h, store_image)
        if o == 1:
            img_to_owners(h)

    def by_row(src, count):
        rows = wide.at[pl.ds(0, count * 8)]
        rows[...] = src[...].astype(jnp.float32).reshape(count * 8, LANES)
        return [wide[pl.ds(r, count, stride=8), :].astype(jnp.bfloat16) for r in range(8)]

    contract = (((1,), (1,)), ((), ()))

    @pl.when(owner)
    def _():
        all_bytes(filt_in, frecv)
        filt = by_row(filt_in, NORB)
        for r in range(8):
            filt_mat[:, r * LANES:(r + 1) * LANES] = filt[r]
        mat = filt_mat[...]
        corr = lax.dot_general(mat, mat, contract, preferred_element_type=jnp.float32)
        for b in range(NBAND):
            rows_out[b, 0] = corr[2 * b:2 * b + 2]
        all_bytes(img_in, irecv)
        img = jnp.concatenate(by_row(img_in, NORB // 2), axis=1)
        proj = lax.dot_general(img, filt_mat[...], contract, preferred_element_type=jnp.float32)
        for j in range(NBAND // 2):
            target = j // 8 * 16 + lax.rem(y + 6 + (j // 2) % 4, 8) * 2 + j % 2
            rows_out[target, 1] = proj[2 * j:2 * j + 2]

        def body(i, _):
            step = image_step(i // 8)
            x_, y_, core_ = lax.rem(x + 2 + (i // 2) % 4, 4), lax.rem(y + 8 - step, 8), lax.rem(core + 1 + i, 2)
            target = x_ * 16 + y_ * 2 + core_
            send_or_keep(rows_out.at[target], rows_in.at[my_chunk], (x_, y_, core_), rsend, rrecv)
            return 0

        lax.fori_loop(0, NBAND // 2, body, 0)

    all_bytes(rows_in, rrecv)
    my_sum[...] = jnp.sum(rows_in[...], axis=0)

    def to_dom(i, _):
        dom_ = lax.rem(dom // 2 * 2 + 4 + i, 8)
        here = jnp.logical_and(same, dom_ == dom)

        @pl.when(here)
        def _():
            pltpu.make_async_copy(my_sum, sums.at[z], drecv).start()

        @pl.when(jnp.logical_not(here))
        def _():
            pltpu.make_async_remote_copy(
                src_ref=my_sum, dst_ref=sums.at[z], send_sem=dsend, recv_sem=drecv,
                device_id=(role, dom_), device_id_type=MESH).start()

        return 0

    lax.fori_loop(0, NDOM, to_dom, 0)
    all_bytes(sums, drecv)
    cell_scale = 1.0 / (PLANES * ROWS * LANES * NDOM)
    out_ref[...] = jnp.sum(sums[...], axis=0) * cell_scale

    for s in range(4):
        for o, h in pieces:
            halo_sent(s, o, h)

    @pl.when(same)
    def _():
        share_pot.wait_send()
        all_bytes(sums.at[pl.ds(0, NDOM - 1)], dsend)

    @pl.when(jnp.logical_not(same))
    def _():
        move(0).wait_send()
        move(1).wait_send()
        all_bytes(sums, dsend)

    @pl.when(owner)
    def _():
        all_bytes(filt_in.at[pl.ds(0, 47)], fsend)
        all_bytes(img_out.at[pl.ds(0, CHUNKS - 1)], isend)
        all_bytes(rows_out.at[pl.ds(0, NBAND // 2 - 1)], rsend)

    @pl.when(jnp.logical_not(owner))
    def _():
        all_bytes(filt_in.at[pl.ds(0, 48)], fsend)
        all_bytes(img_out, isend)


def per_device(orbitals, potential):
    bf16, f32 = jnp.bfloat16, jnp.float32
    dma = pltpu.SemaphoreType.DMA
    out = pl.pallas_call(
        kernel,
        out_shape=jax.ShapeDtypeStruct((2, 2, LANES), f32),
        in_specs=[pl.BlockSpec(memory_space=pltpu.HBM)] * 2,
        out_specs=pl.BlockSpec(memory_space=pltpu.VMEM),
        scratch_shapes=[
            pltpu.VMEM((4, 2, PLANES, ROWS, LANES), bf16),
            pltpu.VMEM((PLANES, ROWS, LANES), f32),
            pltpu.VMEM((4, 2, 2, PLANES, ROWS, LANES), bf16),
            pltpu.VMEM((4, 2, PLANES, ROWS, LANES), f32),
            pltpu.VMEM((2, PLANES, ROWS, LANES), f32),
            pltpu.VMEM((CHUNKS, 2, 8, LANES), bf16),
            pltpu.VMEM((CHUNKS, 2, 8, LANES), bf16),
            pltpu.VMEM((NBAND, 2, 8, LANES), bf16),
            pltpu.VMEM((NBAND // 2, 2, 8, LANES), bf16),
            pltpu.VMEM((NORB * 8, LANES), f32),
            pltpu.VMEM((NORB, 8 * LANES), bf16),
            pltpu.VMEM((NBAND, 2, 2, LANES), f32),
            pltpu.VMEM((CHUNKS, 2, 2, LANES), f32),
            pltpu.VMEM((2, 2, LANES), f32),
            pltpu.VMEM((NDOM, 2, 2, LANES), f32),
            pltpu.SemaphoreType.REGULAR((3,)), dma((2,)), dma((2,)), dma, dma, dma((4, 2, 2, 2)), dma((4, 2, 2, 2)),
            dma, dma, dma, dma, dma, dma, dma, dma,
        ],
        compiler_params=pltpu.CompilerParams(collective_id=0, has_side_effects=True, vmem_limit_bytes=(64 << 20) - (64 << 10)),
    )(orbitals, potential)
    return out[0], out[1]


def solution(mesh):
    placed = (P("band", "dom", None, None), P("dom", None, None))
    return jax.shard_map(
        per_device,
        mesh=mesh,
        in_specs=placed,
        out_specs=(P("band", None), P("band", None)),
        check_vma=False,
    )
```

```python
import jax
import jax.numpy as jnp
from jax import lax
from jax.experimental import pallas as pl
from jax.experimental.pallas import tpu as pltpu
from jax.sharding import PartitionSpec as P

STENCIL = (
    -5369.0 / 1800.0,
    12.0 / 7.0,
    -15.0 / 56.0,
    10.0 / 189.0,
    -1.0 / 112.0,
    2.0 / 1925.0,
    -1.0 / 16632.0,
)
HALF = tuple(-0.5 * w for w in STENCIL)
CENTER = 8.5
SCALE = 1.0 / 5.5
MESH = pl.DeviceIdType.MESH
NBAND, NDOM = 64, 8
PLANES, ROWS, LANES = 6, 32, 128
CHUNKS = 24
NORB = 128


def device_at(x, y, z, core):
    return (x * 8 + y) * 2 + z % 2, z // 2 * 2 + core


def kernel(
    orb_hbm, pot_hbm, out_ref,
    slab, pot, halo, fields, acc, filt_out, img_out, filt_in, img_in, wide, filt_mat, rows_out, rows_in, my_sum, sums,
    relay_sem, own_send, own_recv, pot_send, pot_recv, hsend, hrecv, fsend, frecv, isend, irecv, rsend, rrecv, dsend, drecv,
):
    band = lax.axis_index("band")
    dom = lax.axis_index("dom")
    x, y, zl, core = band // 16, (band // 2) % 8, band % 2, dom % 2
    z = dom // 2 * 2 + zl
    role = x * 16 + y * 2 + core
    same = zl == core
    place = x * 2 + core
    owner = jnp.logical_and(place != 0, place != 5)
    my_chunk = (place - 1 - place // 6) * 4 + y % 4

    def greet(sem, x_, y_, z_, core_):
        pl.semaphore_signal(sem, inc=1, device_id=device_at(lax.rem(x_, 4), lax.rem(y_, 8), lax.rem(z_, 8), core_), device_id_type=MESH)

    barrier = pltpu.get_barrier_semaphore()
    for step in (2, 6, 1, 7):
        for core_ in range(2):
            greet(barrier, x, y, z + step, core_)
    greet(barrier, x, y, z, 1 - core)
    for step in (2, 6, 1, 7):
        greet(barrier, x, y + step, z, core)
    for step in (2, 1, 3):
        greet(barrier, x + step, y, z, core)

    def relay(stage):
        if stage == 0:
            for step in (2, 6):
                greet(relay_sem.at[0], x, y + step, z, core)
                greet(relay_sem.at[0], x, y, z + step, core)
        elif stage == 1:
            pl.semaphore_wait(relay_sem.at[0], 4)
            for step in (2, 1, 3):
                greet(relay_sem.at[1], x + step, y, z, core)
        elif stage == 2:
            pl.semaphore_wait(relay_sem.at[1], 3)
            greet(relay_sem.at[2], x, y, z, 1 - core)
        else:
            pl.semaphore_wait(relay_sem.at[2], 1)

    def load(o):
        return pltpu.make_async_copy(orb_hbm.at[o], slab.at[0, o], own_recv.at[o])

    def move(o):
        return pltpu.make_async_remote_copy(
            src_ref=orb_hbm.at[o], dst_ref=slab.at[0, o], send_sem=own_send.at[o], recv_sem=own_recv.at[o],
            device_id=device_at(x, y, dom, zl), device_id_type=MESH)

    load_pot = pltpu.make_async_copy(pot_hbm, pot, pot_recv)
    share_pot = pltpu.make_async_remote_copy(
        src_ref=pot_hbm, dst_ref=pot, send_sem=pot_send, recv_sem=pot_recv,
        device_id=(band, dom + 1 - 2 * core), device_id_type=MESH)

    @pl.when(same)
    def _():
        load(0).start()
        load(1).start()
        load_pot.start()

    @pl.when(z == 0)
    def _():
        for s in range(4):
            halo[s, 0] = jnp.zeros((2, PLANES, ROWS, LANES), jnp.bfloat16)

    @pl.when(z == NDOM - 1)
    def _():
        for s in range(4):
            halo[s, 1] = jnp.zeros((2, PLANES, ROWS, LANES), jnp.bfloat16)

    def local_part(s, o):
        shift = -CENTER if s < 3 else 0.0

        def body(o, _):
            for p in range(PLANES):
                v = fields[s, o, p]
                total = (pot[p] + (3.0 * HALF[0] + shift)) * v
                for k in range(1, 7):
                    along_y = pltpu.roll(v, k, 0) + pltpu.roll(v, ROWS - k, 0)
                    along_x = pltpu.roll(v, k, 1) + pltpu.roll(v, LANES - k, 1)
                    total = total + HALF[k] * (along_y + along_x)
                for q in range(PLANES):
                    if q != p:
                        total = total + HALF[abs(p - q)] * fields[s, o, q]
                acc[o, p] = total
            return 0

        lax.fori_loop(o, o + 1, body, 0)

    def halo_copies(s, o, h):
        rows = pl.ds(16 * h, 16)
        if s == 0:
            source, at, core_ = orb_hbm.at[o, :, rows, :], dom, zl
        else:
            source, at, core_ = slab.at[s, o, :, rows, :], z, core
        return at, [
            pltpu.make_async_remote_copy(
                src_ref=source, dst_ref=halo.at[s, side, o, :, rows, :],
                send_sem=hsend.at[s, side, o, h], recv_sem=hrecv.at[s, side, o, h],
                device_id=device_at(x, y, lax.rem(at + step, 8), core_), device_id_type=MESH)
            for side, step in ((0, 1), (1, 7))
        ]

    def halo_start(s, o, h):
        at, (up, down) = halo_copies(s, o, h)

        @pl.when(at < NDOM - 1)
        def _():
            up.start()

        @pl.when(at > 0)
        def _():
            down.start()

    def halo_wait(s, o, h):
        _, (up, down) = halo_copies(s, o, h)

        @pl.when(z > 0)
        def _():
            up.wait_recv()

        @pl.when(z < NDOM - 1)
        def _():
            down.wait_recv()

    def halo_sent(s, o, h):
        at, (up, down) = halo_copies(s, o, h)

        @pl.when(at < NDOM - 1)
        def _():
            up.wait_send()

        @pl.when(at > 0)
        def _():
            down.wait_send()

    def halo_part(s, o, h, store):
        rows = pl.ds(16 * h, 16)
        low = [halo[s, 0, o, j, rows, :].astype(jnp.float32) for j in range(PLANES)]
        high = [halo[s, 1, o, j, rows, :].astype(jnp.float32) for j in range(PLANES)]
        for p in range(PLANES):
            total = acc[o, p, rows, :]
            for j in range(p, PLANES):
                total = total + HALF[p + 6 - j] * low[j]
            for j in range(p + 1):
                total = total + HALF[6 + j - p] * high[j]
            store(o, p, h, rows, total)

    def store_field(s):
        def store(o, p, h, rows, total):
            if s == 1:
                value = SCALE * total
            else:
                value = (2.0 * SCALE) * total - fields[s - 2, o, p, rows, :]
            fields[s, o, p, rows, :] = value
            slab[s, o, p, rows, :] = value.astype(jnp.bfloat16)
            if s == 3:
                for t in range(2):
                    filt_out[p * 4 + t * 2 + h, o] = value[8 * t:8 * t + 8].astype(jnp.bfloat16)

        return store

    def store_image(o, p, h, rows, total):
        for t in range(2):
            img_out[p * 4 + t * 2 + h, o] = total[8 * t:8 * t + 8].astype(jnp.bfloat16)

    def send(src, dst, target, send_sem, recv_sem, may_stay):
        x_, y_, core_ = target

        def start():
            pltpu.make_async_remote_copy(
                src_ref=src, dst_ref=dst, send_sem=send_sem, recv_sem=recv_sem,
                device_id=device_at(x_, y_, z, core_), device_id_type=MESH).start()

        if not may_stay:
            start()
            return
        here = jnp.logical_and(y_ == y, x_ * 2 + core_ == place)

        @pl.when(here)
        def _():
            pltpu.make_async_copy(src, dst, recv_sem).start()

        @pl.when(jnp.logical_not(here))
        def _():
            start()

    def to_owners(half, src, dst, slot_of, steps, send_sem, recv_sem):
        odd = (y + half) % 2
        for even_step in steps:
            step = lax.rem(even_step + 8 - odd, 8)
            y_ = lax.rem(y + step, 8)
            slot = slot_of(step)
            for r in range(6):
                place_ = r + 1 + r // 4
                send(src.at[r * 4 + y_ % 4], dst.at[slot], (place_ // 2, y_, place_ % 2), send_sem, recv_sem, even_step == 0)

    def filt_to_owners(half):
        to_owners(half, filt_out, filt_in, lambda step: role, (4, 2, 6, 0), fsend, frecv)

    def img_to_owners(half):
        to_owners(half, img_out, img_in, lambda step: x * 8 + lax.rem(10 - step, 8) * 2 + core, (2, 0), isend, irecv)

    def all_bytes(ref, sem):
        pltpu.make_async_copy(ref, ref, sem).wait()

    pieces = [(o, h) for h in range(2) for o in range(2)]
    pl.semaphore_wait(barrier, 16)

    @pl.when(same)
    def _():
        share_pot.start()

    @pl.when(jnp.logical_not(same))
    def _():
        move(0).start()
        move(1).start()
        for o, h in pieces:
            halo_start(0, o, h)

    relay(0)
    load_pot.wait()
    for o in range(2):
        load(o).wait()
        fields[0, o] = slab[0, o].astype(jnp.float32)
        local_part(0, o)

    @pl.when(same)
    def _():
        for o, h in pieces:
            halo_start(0, o, h)

    relay(1)
    for s in range(3):
        for o, h in pieces:
            halo_wait(s, o, h)
            halo_part(s, o, h, store_field(s + 1))
            halo_start(s + 1, o, h)
            if s == 2 and o == 1:
                filt_to_owners(h)
        for o in range(2):
            local_part(s + 1, o)
        if s < 2:
            relay(s + 2)
    for o, h in pieces:
        halo_wait(3, o, h)
        halo_part(3, o, h, store_image)
        if o == 1:
            img_to_owners(h)

    def by_row(src, count):
        rows = wide.at[pl.ds(0, count * 8)]
        rows[...] = src[...].astype(jnp.float32).reshape(count * 8, LANES)
        return [wide[pl.ds(r, count, stride=8), :].astype(jnp.bfloat16) for r in range(8)]

    contract = (((1,), (1,)), ((), ()))

    @pl.when(owner)
    def _():
        all_bytes(filt_in, frecv)
        filt = by_row(filt_in, NORB)
        for r in range(8):
            filt_mat[:, r * LANES:(r + 1) * LANES] = filt[r]
        mat = filt_mat[...]
        corr = lax.dot_general(mat, mat, contract, preferred_element_type=jnp.float32)
        for b in range(NBAND):
            rows_out[b, 0] = corr[2 * b:2 * b + 2]
        all_bytes(img_in, irecv)
        img = jnp.concatenate(by_row(img_in, NORB // 2), axis=1)
        proj = lax.dot_general(img, filt_mat[...], contract, preferred_element_type=jnp.float32)
        for j in range(NBAND // 2):
            target = j // 8 * 16 + lax.rem(y + 6 + (j // 2) % 4, 8) * 2 + j % 2
            rows_out[target, 1] = proj[2 * j:2 * j + 2]

        for y_step in (6, 1, 7, 0):
            for x_step in (2, 1, 3, 0):
                for core_step in (1, 0):
                    x_, y_, core_ = lax.rem(x + x_step, 4), lax.rem(y + y_step, 8), core_step + core - 2 * core_step * core
                    if x_step + y_step + core_step > 0:
                        send(rows_out.at[x_ * 16 + y_ * 2 + core_], rows_in.at[my_chunk], (x_, y_, core_), rsend, rrecv, False)
        pltpu.make_async_copy(rows_out.at[role], rows_in.at[my_chunk], rrecv).start()

    all_bytes(rows_in, rrecv)
    my_sum[...] = jnp.sum(rows_in[...], axis=0)

    def to_dom(i, _):
        dom_ = lax.rem(dom // 2 * 2 + 4 + i, 8)
        here = jnp.logical_and(same, dom_ == dom)

        @pl.when(here)
        def _():
            pltpu.make_async_copy(my_sum, sums.at[z], drecv).start()

        @pl.when(jnp.logical_not(here))
        def _():
            pltpu.make_async_remote_copy(
                src_ref=my_sum, dst_ref=sums.at[z], send_sem=dsend, recv_sem=drecv,
                device_id=(role, dom_), device_id_type=MESH).start()

        return 0

    lax.fori_loop(0, NDOM, to_dom, 0)
    for s in range(4):
        for o, h in pieces:
            halo_sent(s, o, h)

    @pl.when(same)
    def _():
        share_pot.wait_send()

    @pl.when(jnp.logical_not(same))
    def _():
        move(0).wait_send()
        move(1).wait_send()

    @pl.when(owner)
    def _():
        all_bytes(filt_in.at[pl.ds(0, 47)], fsend)
        all_bytes(img_out.at[pl.ds(0, CHUNKS - 1)], isend)
        all_bytes(rows_out.at[pl.ds(0, NBAND // 2 - 1)], rsend)

    @pl.when(jnp.logical_not(owner))
    def _():
        all_bytes(filt_in.at[pl.ds(0, 48)], fsend)
        all_bytes(img_out, isend)

    all_bytes(sums, drecv)
    cell_scale = 1.0 / (PLANES * ROWS * LANES * NDOM)
    out_ref[...] = jnp.sum(sums[...], axis=0) * cell_scale

    @pl.when(same)
    def _():
        all_bytes(sums.at[pl.ds(0, NDOM - 1)], dsend)

    @pl.when(jnp.logical_not(same))
    def _():
        all_bytes(sums, dsend)


def per_device(orbitals, potential):
    bf16, f32 = jnp.bfloat16, jnp.float32
    dma = pltpu.SemaphoreType.DMA
    out = pl.pallas_call(
        kernel,
        out_shape=jax.ShapeDtypeStruct((2, 2, LANES), f32),
        in_specs=[pl.BlockSpec(memory_space=pltpu.HBM)] * 2,
        out_specs=pl.BlockSpec(memory_space=pltpu.VMEM),
        scratch_shapes=[
            pltpu.VMEM((4, 2, PLANES, ROWS, LANES), bf16),
            pltpu.VMEM((PLANES, ROWS, LANES), f32),
            pltpu.VMEM((4, 2, 2, PLANES, ROWS, LANES), bf16),
            pltpu.VMEM((4, 2, PLANES, ROWS, LANES), f32),
            pltpu.VMEM((2, PLANES, ROWS, LANES), f32),
            pltpu.VMEM((CHUNKS, 2, 8, LANES), bf16),
            pltpu.VMEM((CHUNKS, 2, 8, LANES), bf16),
            pltpu.VMEM((NBAND, 2, 8, LANES), bf16),
            pltpu.VMEM((NBAND // 2, 2, 8, LANES), bf16),
            pltpu.VMEM((NORB * 8, LANES), f32),
            pltpu.VMEM((NORB, 8 * LANES), bf16),
            pltpu.VMEM((NBAND, 2, 2, LANES), f32),
            pltpu.VMEM((CHUNKS, 2, 2, LANES), f32),
            pltpu.VMEM((2, 2, LANES), f32),
            pltpu.VMEM((NDOM, 2, 2, LANES), f32),
            pltpu.SemaphoreType.REGULAR((3,)), dma((2,)), dma((2,)), dma, dma, dma((4, 2, 2, 2)), dma((4, 2, 2, 2)),
            dma, dma, dma, dma, dma, dma, dma, dma,
        ],
        compiler_params=pltpu.CompilerParams(collective_id=0, has_side_effects=True, vmem_limit_bytes=(64 << 20) - (64 << 10)),
    )(orbitals, potential)
    return out[0], out[1]


def solution(mesh):
    placed = (P("band", "dom", None, None), P("dom", None, None))
    return jax.shard_map(
        per_device,
        mesh=mesh,
        in_specs=placed,
        out_specs=(P("band", None), P("band", None)),
        check_vma=False,
    )
```

```python
import jax
import jax.numpy as jnp
from jax import lax
from jax.experimental import pallas as pl
from jax.experimental.pallas import tpu as pltpu
from jax.sharding import PartitionSpec as P

STENCIL = (
    -5369.0 / 1800.0,
    12.0 / 7.0,
    -15.0 / 56.0,
    10.0 / 189.0,
    -1.0 / 112.0,
    2.0 / 1925.0,
    -1.0 / 16632.0,
)
HALF = tuple(-0.5 * w for w in STENCIL)
CENTER = 8.5
SCALE = 1.0 / 5.5
MESH = pl.DeviceIdType.MESH
NBAND, NDOM = 64, 8
PLANES, ROWS, LANES = 6, 32, 128
CHUNKS = 24
NORB = 128


def device_at(x, y, z, core):
    return (x * 8 + y) * 2 + z % 2, z // 2 * 2 + core


def kernel(
    orb_hbm, pot_hbm, out_ref,
    mine, slab, pot, halo, fields, acc, filt_out, img_out, filt_in, img_in, wide, filt_mat, rows_out, rows_in, my_sum, sums,
    relay_sem, load_sem, own_send, own_recv, pot_send, pot_recv, hsend, hrecv, fsend, frecv, isend, irecv, rsend, rrecv, dsend, drecv,
):
    band = lax.axis_index("band")
    dom = lax.axis_index("dom")
    x, y, zl, core = band // 16, (band // 2) % 8, band % 2, dom % 2
    z = dom // 2 * 2 + zl
    role = x * 16 + y * 2 + core
    same = zl == core
    place = x * 2 + core
    owner = jnp.logical_and(place != 0, place != 5)
    my_chunk = (place - 1 - place // 6) * 4 + y % 4

    def greet(sem, x_, y_, z_, core_):
        pl.semaphore_signal(sem, inc=1, device_id=device_at(lax.rem(x_, 4), lax.rem(y_, 8), lax.rem(z_, 8), core_), device_id_type=MESH)

    barrier = pltpu.get_barrier_semaphore()
    for step in (2, 6, 1, 7):
        for core_ in range(2):
            greet(barrier, x, y, z + step, core_)
    greet(barrier, x, y, z, 1 - core)
    for step in (2, 6, 1, 7):
        greet(barrier, x, y + step, z, core)
    for step in (2, 1, 3):
        greet(barrier, x + step, y, z, core)

    def relay(stage):
        if stage == 0:
            for step in (2, 6):
                greet(relay_sem.at[0], x, y + step, z, core)
                greet(relay_sem.at[0], x, y, z + step, core)
        elif stage == 1:
            pl.semaphore_wait(relay_sem.at[0], 4)
            for step in (2, 1, 3):
                greet(relay_sem.at[1], x + step, y, z, core)
        elif stage == 2:
            pl.semaphore_wait(relay_sem.at[1], 3)
            greet(relay_sem.at[2], x, y, z, 1 - core)
        else:
            pl.semaphore_wait(relay_sem.at[2], 1)

    load = pltpu.make_async_copy(orb_hbm, mine, load_sem)
    load.start()

    def move(o):
        return pltpu.make_async_remote_copy(
            src_ref=mine.at[o], dst_ref=slab.at[0, o], send_sem=own_send.at[o], recv_sem=own_recv.at[o],
            device_id=device_at(x, y, dom, zl), device_id_type=MESH)

    load_pot = pltpu.make_async_copy(pot_hbm, pot, pot_recv)
    share_pot = pltpu.make_async_remote_copy(
        src_ref=pot, dst_ref=pot, send_sem=pot_send, recv_sem=pot_recv,
        device_id=(band, dom + 1 - 2 * core), device_id_type=MESH)

    @pl.when(same)
    def _():
        load_pot.start()

    @pl.when(z == 0)
    def _():
        for s in range(4):
            halo[s, 0] = jnp.zeros((2, PLANES, ROWS, LANES), jnp.bfloat16)

    @pl.when(z == NDOM - 1)
    def _():
        for s in range(4):
            halo[s, 1] = jnp.zeros((2, PLANES, ROWS, LANES), jnp.bfloat16)

    def local_part(s, o):
        shift = -CENTER if s < 3 else 0.0

        def body(o, _):
            for p in range(PLANES):
                v = fields[s, o, p]
                total = (pot[p] + (3.0 * HALF[0] + shift)) * v
                for k in range(1, 7):
                    along_y = pltpu.roll(v, k, 0) + pltpu.roll(v, ROWS - k, 0)
                    along_x = pltpu.roll(v, k, 1) + pltpu.roll(v, LANES - k, 1)
                    total = total + HALF[k] * (along_y + along_x)
                for q in range(PLANES):
                    if q != p:
                        total = total + HALF[abs(p - q)] * fields[s, o, q]
                acc[o, p] = total
            return 0

        lax.fori_loop(o, o + 1, body, 0)

    def halo_copies(s, o, h):
        rows = pl.ds(16 * h, 16)
        if s == 0:
            source, at, core_ = mine.at[o, :, rows, :], dom, zl
        else:
            source, at, core_ = slab.at[s, o, :, rows, :], z, core
        return at, [
            pltpu.make_async_remote_copy(
                src_ref=source, dst_ref=halo.at[s, side, o, :, rows, :],
                send_sem=hsend.at[s, side, o, h], recv_sem=hrecv.at[s, side, o, h],
                device_id=device_at(x, y, lax.rem(at + step, 8), core_), device_id_type=MESH)
            for side, step in ((0, 1), (1, 7))
        ]

    def halo_start(s, o, h):
        at, (up, down) = halo_copies(s, o, h)

        @pl.when(at < NDOM - 1)
        def _():
            up.start()

        @pl.when(at > 0)
        def _():
            down.start()

    def halo_wait(s, o, h):
        _, (up, down) = halo_copies(s, o, h)

        @pl.when(z > 0)
        def _():
            up.wait_recv()

        @pl.when(z < NDOM - 1)
        def _():
            down.wait_recv()

    def halo_sent(s, o, h):
        at, (up, down) = halo_copies(s, o, h)

        @pl.when(at < NDOM - 1)
        def _():
            up.wait_send()

        @pl.when(at > 0)
        def _():
            down.wait_send()

    def halo_part(s, o, h, store):
        rows = pl.ds(16 * h, 16)
        low = [halo[s, 0, o, j, rows, :].astype(jnp.float32) for j in range(PLANES)]
        high = [halo[s, 1, o, j, rows, :].astype(jnp.float32) for j in range(PLANES)]
        for p in range(PLANES):
            total = acc[o, p, rows, :]
            for j in range(p, PLANES):
                total = total + HALF[p + 6 - j] * low[j]
            for j in range(p + 1):
                total = total + HALF[6 + j - p] * high[j]
            store(o, p, h, rows, total)

    def store_field(s):
        def store(o, p, h, rows, total):
            if s == 1:
                value = SCALE * total
            else:
                value = (2.0 * SCALE) * total - fields[s - 2, o, p, rows, :]
            fields[s, o, p, rows, :] = value
            slab[s, o, p, rows, :] = value.astype(jnp.bfloat16)
            if s == 3:
                for t in range(2):
                    filt_out[p * 4 + t * 2 + h, o] = value[8 * t:8 * t + 8].astype(jnp.bfloat16)

        return store

    def store_image(o, p, h, rows, total):
        for t in range(2):
            img_out[p * 4 + t * 2 + h, o] = total[8 * t:8 * t + 8].astype(jnp.bfloat16)

    def send(src, dst, target, send_sem, recv_sem, may_stay):
        x_, y_, core_ = target

        def start():
            pltpu.make_async_remote_copy(
                src_ref=src, dst_ref=dst, send_sem=send_sem, recv_sem=recv_sem,
                device_id=device_at(x_, y_, z, core_), device_id_type=MESH).start()

        if not may_stay:
            start()
            return
        here = jnp.logical_and(y_ == y, x_ * 2 + core_ == place)

        @pl.when(here)
        def _():
            pltpu.make_async_copy(src, dst, recv_sem).start()

        @pl.when(jnp.logical_not(here))
        def _():
            start()

    def to_owners(half, src, dst, slot_of, steps, send_sem, recv_sem):
        odd = (y + half) % 2
        for even_step in steps:
            step = lax.rem(even_step + 8 - odd, 8)
            y_ = lax.rem(y + step, 8)
            for r in range(6):
                place_ = r + 1 + r // 4
                slot = slot_of(place_ // 2, step)
                send(src.at[r * 4 + y_ % 4], dst.at[slot], (place_ // 2, y_, place_ % 2), send_sem, recv_sem, even_step == 0)

    def filt_to_owners(half):
        to_owners(half, filt_out, filt_in, lambda x_, step: role, (4, 2, 6, 0), fsend, frecv)

    def img_to_owners(half):
        to_owners(half, img_out, img_in, lambda x_, step: lax.rem(x + 4 - x_, 4) * 8 + lax.rem(10 - step, 8) * 2 + core,
                  (2, 0), isend, irecv)

    def all_bytes(ref, sem):
        pltpu.make_async_copy(ref, ref, sem).wait()

    pieces = [(o, h) for h in range(2) for o in range(2)]
    load.wait()

    @pl.when(same)
    def _():
        load_pot.wait()

    pl.semaphore_wait(barrier, 16)

    @pl.when(same)
    def _():
        share_pot.start()

    @pl.when(jnp.logical_not(same))
    def _():
        move(0).start()
        move(1).start()

    for o, h in pieces:
        halo_start(0, o, h)
    relay(0)

    @pl.when(jnp.logical_not(same))
    def _():
        share_pot.wait_recv()

    for o in range(2):
        @pl.when(same)
        def _():
            fields[0, o] = mine[o].astype(jnp.float32)

        @pl.when(jnp.logical_not(same))
        def _():
            move(o).wait_recv()
            fields[0, o] = slab[0, o].astype(jnp.float32)

        local_part(0, o)
    relay(1)
    for s in range(3):
        for o, h in pieces:
            halo_wait(s, o, h)
            halo_part(s, o, h, store_field(s + 1))
            halo_start(s + 1, o, h)
            if s == 2 and o == 1:
                filt_to_owners(h)
        for o in range(2):
            local_part(s + 1, o)
        if s < 2:
            relay(s + 2)
    for o, h in pieces:
        halo_wait(3, o, h)
        halo_part(3, o, h, store_image)
        if o == 1:
            img_to_owners(h)

    def by_row(src, count):
        rows = wide.at[pl.ds(0, count * 8)]
        rows[...] = src[...].astype(jnp.float32).reshape(count * 8, LANES)
        return [wide[pl.ds(r, count, stride=8), :].astype(jnp.bfloat16) for r in range(8)]

    contract = (((1,), (1,)), ((), ()))

    @pl.when(owner)
    def _():
        all_bytes(filt_in, frecv)
        filt = by_row(filt_in, NORB)
        for r in range(8):
            filt_mat[:, r * LANES:(r + 1) * LANES] = filt[r]
        mat = filt_mat[...]
        corr = lax.dot_general(mat, mat, contract, preferred_element_type=jnp.float32)
        for b in range(NBAND):
            rows_out[b, 0] = corr[2 * b:2 * b + 2]
        all_bytes(img_in, irecv)
        img = jnp.concatenate(by_row(img_in, NORB // 2), axis=1)
        proj = lax.dot_general(img, filt_mat[...], contract, preferred_element_type=jnp.float32)
        for y_step in (6, 1, 7, 0):
            for x_step in (2, 1, 3, 0):
                for core_ in range(2):
                    x_, y_ = lax.rem(x + x_step, 4), lax.rem(y + y_step, 8)
                    target, j = x_ * 16 + y_ * 2 + core_, x_step * 8 + (y_step + 2) % 8 * 2 + core_
                    rows_out[target, 1] = proj[2 * j:2 * j + 2]
                    send(rows_out.at[target], rows_in.at[my_chunk], (x_, y_, core_), rsend, rrecv, x_step + y_step == 0)

    all_bytes(rows_in, rrecv)
    my_sum[...] = jnp.sum(rows_in[...], axis=0)

    def to_dom(i):
        here = jnp.logical_and(same, i == dom)

        @pl.when(here)
        def _():
            pltpu.make_async_copy(my_sum, sums.at[z], drecv).start()

        @pl.when(jnp.logical_not(here))
        def _():
            pltpu.make_async_remote_copy(
                src_ref=my_sum, dst_ref=sums.at[z], send_sem=dsend, recv_sem=drecv,
                device_id=(role, i), device_id_type=MESH).start()

    for i in range(NDOM):
        to_dom(i)

    for s in range(4):
        for o, h in pieces:
            halo_sent(s, o, h)

    @pl.when(same)
    def _():
        share_pot.wait_send()

    @pl.when(jnp.logical_not(same))
    def _():
        move(0).wait_send()
        move(1).wait_send()

    @pl.when(owner)
    def _():
        all_bytes(filt_in.at[pl.ds(0, 47)], fsend)
        all_bytes(img_out.at[pl.ds(0, CHUNKS - 1)], isend)
        all_bytes(rows_out.at[pl.ds(0, NBAND // 2 - 1)], rsend)

    @pl.when(jnp.logical_not(owner))
    def _():
        all_bytes(filt_in.at[pl.ds(0, 48)], fsend)
        all_bytes(img_out, isend)

    all_bytes(sums, drecv)
    cell_scale = 1.0 / (PLANES * ROWS * LANES * NDOM)
    out_ref[...] = jnp.sum(sums[...], axis=0) * cell_scale

    @pl.when(same)
    def _():
        all_bytes(sums.at[pl.ds(0, NDOM - 1)], dsend)

    @pl.when(jnp.logical_not(same))
    def _():
        all_bytes(sums, dsend)


def per_device(orbitals, potential):
    bf16, f32 = jnp.bfloat16, jnp.float32
    dma = pltpu.SemaphoreType.DMA
    out = pl.pallas_call(
        kernel,
        out_shape=jax.ShapeDtypeStruct((2, 2, LANES), f32),
        in_specs=[pl.BlockSpec(memory_space=pltpu.HBM)] * 2,
        out_specs=pl.BlockSpec(memory_space=pltpu.VMEM),
        scratch_shapes=[
            pltpu.VMEM((2, PLANES, ROWS, LANES), bf16),
            pltpu.VMEM((4, 2, PLANES, ROWS, LANES), bf16),
            pltpu.VMEM((PLANES, ROWS, LANES), f32),
            pltpu.VMEM((4, 2, 2, PLANES, ROWS, LANES), bf16),
            pltpu.VMEM((4, 2, PLANES, ROWS, LANES), f32),
            pltpu.VMEM((2, PLANES, ROWS, LANES), f32),
            pltpu.VMEM((CHUNKS, 2, 8, LANES), bf16),
            pltpu.VMEM((CHUNKS, 2, 8, LANES), bf16),
            pltpu.VMEM((NBAND, 2, 8, LANES), bf16),
            pltpu.VMEM((NBAND // 2, 2, 8, LANES), bf16),
            pltpu.VMEM((NORB * 8, LANES), f32),
            pltpu.VMEM((NORB, 8 * LANES), bf16),
            pltpu.VMEM((NBAND, 2, 2, LANES), f32),
            pltpu.VMEM((CHUNKS, 2, 2, LANES), f32),
            pltpu.VMEM((2, 2, LANES), f32),
            pltpu.VMEM((NDOM, 2, 2, LANES), f32),
            pltpu.SemaphoreType.REGULAR((3,)), dma, dma((2,)), dma((2,)), dma, dma, dma((4, 2, 2, 2)), dma((4, 2, 2, 2)),
            dma, dma, dma, dma, dma, dma, dma, dma,
        ],
        compiler_params=pltpu.CompilerParams(collective_id=0, has_side_effects=True, vmem_limit_bytes=(64 << 20) - (64 << 10)),
    )(orbitals, potential)
    return out[0], out[1]


def solution(mesh):
    placed = (P("band", "dom", None, None), P("dom", None, None))
    return jax.shard_map(
        per_device,
        mesh=mesh,
        in_specs=placed,
        out_specs=(P("band", None), P("band", None)),
        check_vma=False,
    )
```

```python
import jax
import jax.numpy as jnp
from jax import lax
from jax.experimental import pallas as pl
from jax.experimental.pallas import tpu as pltpu
from jax.sharding import PartitionSpec as P

STENCIL = (
    -5369.0 / 1800.0,
    12.0 / 7.0,
    -15.0 / 56.0,
    10.0 / 189.0,
    -1.0 / 112.0,
    2.0 / 1925.0,
    -1.0 / 16632.0,
)
HALF = tuple(-0.5 * w for w in STENCIL)
CENTER = 8.5
SCALE = 1.0 / 5.5
MESH = pl.DeviceIdType.MESH
NBAND, NDOM = 64, 8
PLANES, ROWS, LANES = 6, 32, 128
CHUNKS = 24
NORB = 128


def device_at(x, y, z, core):
    return (x * 8 + y) * 2 + z % 2, z // 2 * 2 + core


def kernel(
    orb_hbm, pot_hbm, out_ref,
    mine, slab, pot, halo, fields, acc, filt_out, img_out, filt_in, img_in, wide, filt_mat, rows_out, rows_in, my_sum, sums,
    relay_sem, load_sem, own_send, own_recv, pot_send, pot_recv, hsend, hrecv, fsend, frecv, isend, irecv, rsend, rrecv, dsend, drecv,
):
    band = lax.axis_index("band")
    dom = lax.axis_index("dom")
    x, y, zl, core = band // 16, (band // 2) % 8, band % 2, dom % 2
    z = dom // 2 * 2 + zl
    role = x * 16 + y * 2 + core
    same = zl == core
    place = x * 2 + core
    owner = jnp.logical_and(place != 0, place != 5)
    my_chunk = (place - 1 - place // 6) * 4 + y % 4

    def greet(sem, x_, y_, z_, core_):
        pl.semaphore_signal(sem, inc=1, device_id=device_at(lax.rem(x_, 4), lax.rem(y_, 8), lax.rem(z_, 8), core_), device_id_type=MESH)

    barrier = pltpu.get_barrier_semaphore()
    for step in (2, 6, 1, 7):
        for core_ in range(2):
            greet(barrier, x, y, z + step, core_)
    greet(barrier, x, y, z, 1 - core)
    for step in (2, 6, 1, 7):
        greet(barrier, x, y + step, z, core)
    for step in (2, 1, 3):
        greet(barrier, x + step, y, z, core)

    def relay(stage):
        if stage == 0:
            for step in (2, 6):
                greet(relay_sem.at[0], x, y + step, z, core)
                greet(relay_sem.at[0], x, y, z + step, core)
        elif stage == 1:
            pl.semaphore_wait(relay_sem.at[0], 4)
            for step in (2, 1, 3):
                greet(relay_sem.at[1], x + step, y, z, core)
        elif stage == 2:
            pl.semaphore_wait(relay_sem.at[1], 3)
            greet(relay_sem.at[2], x, y, z, 1 - core)
        else:
            pl.semaphore_wait(relay_sem.at[2], 1)

    load = pltpu.make_async_copy(orb_hbm, mine, load_sem)
    load.start()

    def move(o):
        return pltpu.make_async_remote_copy(
            src_ref=mine.at[o], dst_ref=slab.at[0, o], send_sem=own_send.at[o], recv_sem=own_recv.at[o],
            device_id=device_at(x, y, dom, zl), device_id_type=MESH)

    load_pot = pltpu.make_async_copy(pot_hbm, pot, pot_recv)
    share_pot = pltpu.make_async_remote_copy(
        src_ref=pot, dst_ref=pot, send_sem=pot_send, recv_sem=pot_recv,
        device_id=(band, dom + 1 - 2 * core), device_id_type=MESH)

    @pl.when(same)
    def _():
        load_pot.start()

    @pl.when(z == 0)
    def _():
        for s in range(4):
            halo[s, 0] = jnp.zeros((2, PLANES, ROWS, LANES), jnp.bfloat16)

    @pl.when(z == NDOM - 1)
    def _():
        for s in range(4):
            halo[s, 1] = jnp.zeros((2, PLANES, ROWS, LANES), jnp.bfloat16)

    def local_part(s, o):
        shift = -CENTER if s < 3 else 0.0

        def body(o, _):
            for p in range(PLANES):
                v = fields[s, o, p]
                total = (pot[p] + (3.0 * HALF[0] + shift)) * v
                for k in range(1, 7):
                    along_y = pltpu.roll(v, k, 0) + pltpu.roll(v, ROWS - k, 0)
                    along_x = pltpu.roll(v, k, 1) + pltpu.roll(v, LANES - k, 1)
                    total = total + HALF[k] * (along_y + along_x)
                for q in range(PLANES):
                    if q != p:
                        total = total + HALF[abs(p - q)] * fields[s, o, q]
                acc[o, p] = total
            return 0

        lax.fori_loop(o, o + 1, body, 0)

    def halo_copies(s, o, h):
        rows = pl.ds(16 * h, 16)
        if s == 0:
            source, at, core_ = mine.at[o, :, rows, :], dom, zl
        else:
            source, at, core_ = slab.at[s, o, :, rows, :], z, core
        return at, [
            pltpu.make_async_remote_copy(
                src_ref=source, dst_ref=halo.at[s, side, o, :, rows, :],
                send_sem=hsend.at[s, side, o, h], recv_sem=hrecv.at[s, side, o, h],
                device_id=device_at(x, y, lax.rem(at + step, 8), core_), device_id_type=MESH)
            for side, step in ((0, 1), (1, 7))
        ]

    def halo_start(s, o, h):
        at, (up, down) = halo_copies(s, o, h)

        @pl.when(at < NDOM - 1)
        def _():
            up.start()

        @pl.when(at > 0)
        def _():
            down.start()

    def halo_wait(s, o, h):
        _, (up, down) = halo_copies(s, o, h)

        @pl.when(z > 0)
        def _():
            up.wait_recv()

        @pl.when(z < NDOM - 1)
        def _():
            down.wait_recv()

    def halo_sent(s, o, h):
        at, (up, down) = halo_copies(s, o, h)

        @pl.when(at < NDOM - 1)
        def _():
            up.wait_send()

        @pl.when(at > 0)
        def _():
            down.wait_send()

    def halo_part(s, o, h, store):
        rows = pl.ds(16 * h, 16)
        low = [halo[s, 0, o, j, rows, :].astype(jnp.float32) for j in range(PLANES)]
        high = [halo[s, 1, o, j, rows, :].astype(jnp.float32) for j in range(PLANES)]
        for p in range(PLANES):
            total = acc[o, p, rows, :]
            for j in range(p, PLANES):
                total = total + HALF[p + 6 - j] * low[j]
            for j in range(p + 1):
                total = total + HALF[6 + j - p] * high[j]
            store(o, p, h, rows, total)

    def store_field(s):
        def store(o, p, h, rows, total):
            if s == 1:
                value = SCALE * total
            else:
                value = (2.0 * SCALE) * total - fields[s - 2, o, p, rows, :]
            fields[s, o, p, rows, :] = value
            slab[s, o, p, rows, :] = value.astype(jnp.bfloat16)
            if s == 3:
                for t in range(2):
                    filt_out[p * 4 + t * 2 + h, o] = value[8 * t:8 * t + 8].astype(jnp.bfloat16)

        return store

    def store_image(o, p, h, rows, total):
        for t in range(2):
            img_out[p * 4 + t * 2 + h, o] = total[8 * t:8 * t + 8].astype(jnp.bfloat16)

    def send(src, dst, target, send_sem, recv_sem, may_stay):
        x_, y_, core_ = target

        def start():
            pltpu.make_async_remote_copy(
                src_ref=src, dst_ref=dst, send_sem=send_sem, recv_sem=recv_sem,
                device_id=device_at(x_, y_, z, core_), device_id_type=MESH).start()

        if not may_stay:
            start()
            return
        here = jnp.logical_and(y_ == y, x_ * 2 + core_ == place)

        @pl.when(here)
        def _():
            pltpu.make_async_copy(src, dst, recv_sem).start()

        @pl.when(jnp.logical_not(here))
        def _():
            start()

    def to_owners(half, src, dst, slot_of, steps, send_sem, recv_sem):
        odd = (y + half) % 2
        for even_step in steps:
            step = lax.rem(even_step + 8 - odd, 8)
            y_ = lax.rem(y + step, 8)
            for r in range(6):
                place_ = r + 1 + r // 4
                slot = slot_of(place_ // 2, step)
                send(src.at[r * 4 + y_ % 4], dst.at[slot], (place_ // 2, y_, place_ % 2), send_sem, recv_sem(even_step), even_step == 0)

    def filt_to_owners(half):
        to_owners(half, filt_out, filt_in, lambda x_, step: role, (4, 2, 6, 0), fsend, lambda even_step: frecv)

    def img_to_owners(half):
        to_owners(half, img_out, img_in, lambda x_, step: lax.rem(10 - step, 8) * 8 + lax.rem(x + 4 - x_, 4) * 2 + core,
                  (2, 0), isend, lambda even_step: irecv.at[1 - even_step // 2])

    def all_bytes(ref, sem):
        pltpu.make_async_copy(ref, ref, sem).wait()

    pieces = [(o, h) for h in range(2) for o in range(2)]
    load.wait()

    @pl.when(same)
    def _():
        load_pot.wait()

    pl.semaphore_wait(barrier, 16)

    @pl.when(same)
    def _():
        share_pot.start()

    @pl.when(jnp.logical_not(same))
    def _():
        move(0).start()
        move(1).start()

    for o, h in pieces:
        halo_start(0, o, h)
    relay(0)

    @pl.when(jnp.logical_not(same))
    def _():
        share_pot.wait_recv()

    for o in range(2):
        @pl.when(same)
        def _():
            fields[0, o] = mine[o].astype(jnp.float32)

        @pl.when(jnp.logical_not(same))
        def _():
            move(o).wait_recv()
            fields[0, o] = slab[0, o].astype(jnp.float32)

        local_part(0, o)
    relay(1)
    for s in range(3):
        for o, h in pieces:
            halo_wait(s, o, h)
            halo_part(s, o, h, store_field(s + 1))
            halo_start(s + 1, o, h)
            if s == 2 and o == 1:
                filt_to_owners(h)
        for o in range(2):
            local_part(s + 1, o)
        if s < 2:
            relay(s + 2)
    for o, h in pieces:
        halo_wait(3, o, h)
        halo_part(3, o, h, store_image)
        if o == 1:
            img_to_owners(h)

    def by_row(src, count):
        rows = wide.at[pl.ds(0, count * 8)]
        rows[...] = src[...].astype(jnp.float32).reshape(count * 8, LANES)
        return [wide[pl.ds(r, count, stride=8), :].astype(jnp.bfloat16) for r in range(8)]

    contract = (((1,), (1,)), ((), ()))

    @pl.when(owner)
    def _():
        all_bytes(filt_in, frecv)
        filt = by_row(filt_in, NORB)
        for r in range(8):
            filt_mat[:, r * LANES:(r + 1) * LANES] = filt[r]
        mat = filt_mat[...]
        corr = lax.dot_general(mat, mat, contract, preferred_element_type=jnp.float32)
        for b in range(NBAND):
            rows_out[b, 0] = corr[2 * b:2 * b + 2]
        for group in (1, 0):
            group_in = img_in.at[pl.ds(16 * group, 16)]
            all_bytes(group_in, irecv.at[group])
            img = jnp.concatenate(by_row(group_in, NORB // 4), axis=1)
            proj = lax.dot_general(img, filt_mat[...], contract, preferred_element_type=jnp.float32)
            for y_step in ((6, 7), (1, 0))[group]:
                for x_step in (2, 1, 3, 0):
                    for core_ in range(2):
                        x_, y_ = lax.rem(x + x_step, 4), lax.rem(y + y_step, 8)
                        target, j = x_ * 16 + y_ * 2 + core_, y_step % 2 * 8 + x_step * 2 + core_
                        rows_out[target, 1] = proj[2 * j:2 * j + 2]
                        send(rows_out.at[target], rows_in.at[my_chunk], (x_, y_, core_), rsend, rrecv, x_step + y_step == 0)

    all_bytes(rows_in, rrecv)
    my_sum[...] = jnp.sum(rows_in[...], axis=0)

    def to_dom(i):
        here = jnp.logical_and(same, i == dom)

        @pl.when(here)
        def _():
            pltpu.make_async_copy(my_sum, sums.at[z], drecv).start()

        @pl.when(jnp.logical_not(here))
        def _():
            pltpu.make_async_remote_copy(
                src_ref=my_sum, dst_ref=sums.at[z], send_sem=dsend, recv_sem=drecv,
                device_id=(role, i), device_id_type=MESH).start()

    for i in range(NDOM):
        to_dom(i)

    for s in range(4):
        for o, h in pieces:
            halo_sent(s, o, h)

    @pl.when(same)
    def _():
        share_pot.wait_send()

    @pl.when(jnp.logical_not(same))
    def _():
        move(0).wait_send()
        move(1).wait_send()

    @pl.when(owner)
    def _():
        all_bytes(filt_in.at[pl.ds(0, 47)], fsend)
        all_bytes(img_out.at[pl.ds(0, CHUNKS - 1)], isend)
        all_bytes(rows_out.at[pl.ds(0, NBAND // 2 - 1)], rsend)

    @pl.when(jnp.logical_not(owner))
    def _():
        all_bytes(filt_in.at[pl.ds(0, 48)], fsend)
        all_bytes(img_out, isend)

    all_bytes(sums, drecv)
    cell_scale = 1.0 / (PLANES * ROWS * LANES * NDOM)
    out_ref[...] = jnp.sum(sums[...], axis=0) * cell_scale

    @pl.when(same)
    def _():
        all_bytes(sums.at[pl.ds(0, NDOM - 1)], dsend)

    @pl.when(jnp.logical_not(same))
    def _():
        all_bytes(sums, dsend)


def per_device(orbitals, potential):
    bf16, f32 = jnp.bfloat16, jnp.float32
    dma = pltpu.SemaphoreType.DMA
    out = pl.pallas_call(
        kernel,
        out_shape=jax.ShapeDtypeStruct((2, 2, LANES), f32),
        in_specs=[pl.BlockSpec(memory_space=pltpu.HBM)] * 2,
        out_specs=pl.BlockSpec(memory_space=pltpu.VMEM),
        scratch_shapes=[
            pltpu.VMEM((2, PLANES, ROWS, LANES), bf16),
            pltpu.VMEM((4, 2, PLANES, ROWS, LANES), bf16),
            pltpu.VMEM((PLANES, ROWS, LANES), f32),
            pltpu.VMEM((4, 2, 2, PLANES, ROWS, LANES), bf16),
            pltpu.VMEM((4, 2, PLANES, ROWS, LANES), f32),
            pltpu.VMEM((2, PLANES, ROWS, LANES), f32),
            pltpu.VMEM((CHUNKS, 2, 8, LANES), bf16),
            pltpu.VMEM((CHUNKS, 2, 8, LANES), bf16),
            pltpu.VMEM((NBAND, 2, 8, LANES), bf16),
            pltpu.VMEM((NBAND // 2, 2, 8, LANES), bf16),
            pltpu.VMEM((NORB * 8, LANES), f32),
            pltpu.VMEM((NORB, 8 * LANES), bf16),
            pltpu.VMEM((NBAND, 2, 2, LANES), f32),
            pltpu.VMEM((CHUNKS, 2, 2, LANES), f32),
            pltpu.VMEM((2, 2, LANES), f32),
            pltpu.VMEM((NDOM, 2, 2, LANES), f32),
            pltpu.SemaphoreType.REGULAR((3,)), dma, dma((2,)), dma((2,)), dma, dma, dma((4, 2, 2, 2)), dma((4, 2, 2, 2)),
            dma, dma, dma, dma((2,)), dma, dma, dma, dma,
        ],
        compiler_params=pltpu.CompilerParams(collective_id=0, has_side_effects=True, vmem_limit_bytes=(64 << 20) - (64 << 10)),
    )(orbitals, potential)
    return out[0], out[1]


def solution(mesh):
    placed = (P("band", "dom", None, None), P("dom", None, None))
    return jax.shard_map(
        per_device,
        mesh=mesh,
        in_specs=placed,
        out_specs=(P("band", None), P("band", None)),
        check_vma=False,
    )
```
